32 devices in a mesh: seq: 8 (over z, y), sub: 4 (over x, core).
Axes of the slice: x: 2, y: 2, z: 4, core: 2. Of those that a mesh axis runs over, the one named last changes fastest.
Arguments:
- queries: bfloat16 [4096, 1024], P(('seq', 'sub')), may hold values from -6 to 6
- key_vectors: bfloat16 [4096, 1024], P(('seq', 'sub')), may hold values from -6 to 6
- values: bfloat16 [4096, 2048], P(('seq', 'sub')), may hold values from -6 to 6
- log_decay: float32 [16, 4096], P(None, ('seq', 'sub')), may hold values from -0.85 to 0, as said below
- write_rate: float32 [16, 4096], P(None, ('seq', 'sub')), may hold values from 0 to 1
- passage_lengths: int32 [8], replicated, may hold values from 1 to 2048, 4096 in all
- norm_gain: float32 [128], replicated, may hold values from 0.1 to 1.9
Outputs:
- head_outputs: bfloat16 [4096, 2048], P(('seq', 'sub'))
The draws below stay inside these ranges and needn't reach their ends.
Inputs may be any that keep to these rules, and one draw needn't show every extreme that they name: `passage_lengths`: 8 segment lengths that add up to 4096; the longest holds exactly 2048 tokens. `log_decay`: never positive.
All inputs are finite; a program needn't handle non-finite values.
Results may differ from the reference program's by a relative error of at most 0.001.
Values sent between devices are 32-bit elements; how exact they have to be, the bound alone decides.
No kernel may reach another device: no remote copies, remote signals or barrier semaphores. Data moves between devices by JAX's collectives and lax.ppermute only.
A program may use at most 192 MiB of HBM per device.

```python
import math
import jax
import jax.numpy as jnp
import numpy as np
from jax import lax

D_K = 128
D_V = 128
VALUE_HEADS = 16
HK = 8
TOK_DEV = 128
PROMPT_TOKENS = 4096
NPASS = 8
SEGMENT_LONGEST = 2048


def head_classes(key, fast_share):
    fast_mask = jax.random.uniform(jax.random.fold_in(key, 11), (VALUE_HEADS,)) < fast_share
    head_order = jax.random.permutation(jax.random.fold_in(key, 13), VALUE_HEADS)
    ranked = jnp.where(fast_mask, VALUE_HEADS + head_order, head_order)
    second_rank = jnp.sort(ranked)[min(1, VALUE_HEADS - 1)]
    medium_mask = jnp.logical_not(fast_mask) & (ranked <= second_rank)
    return (fast_mask, medium_mask)


def draw_log_decay(key, part):
    fast_mask, medium_mask = head_classes(key, 0.5)
    key = jax.random.fold_in(key, 23)
    random_child_keys = jax.random.split(key, 7)
    fast_rate = 1.0 / jax.random.uniform(random_child_keys[0], (VALUE_HEADS,), minval=30.0, maxval=50.0)
    slow_rate = jax.random.uniform(random_child_keys[1], (VALUE_HEADS,), minval=0.05, maxval=0.5) / SEGMENT_LONGEST
    medium_rate = 1.0 / jax.random.uniform(random_child_keys[6], (VALUE_HEADS,), minval=230.0, maxval=320.0)
    baseline_rate = jnp.where(fast_mask, fast_rate, jnp.where(medium_mask, medium_rate, slow_rate))
    rate_dispersion = jnp.exp(jax.random.uniform(random_child_keys[2], (VALUE_HEADS, PROMPT_TOKENS // TOK_DEV), minval=-0.7, maxval=0.7))
    rate_dispersion = jnp.repeat(rate_dispersion, TOK_DEV, axis=1)
    jitter_amount = jax.random.uniform(random_child_keys[3], (VALUE_HEADS, PROMPT_TOKENS), minval=0.5, maxval=1.5)
    surge_events = jax.random.uniform(random_child_keys[4], (VALUE_HEADS, PROMPT_TOKENS)) < 1.0 / SEGMENT_LONGEST
    surge_decay_drops = jnp.log(jax.random.uniform(random_child_keys[5], (VALUE_HEADS, PROMPT_TOKENS), minval=0.5, maxval=0.8))
    return (-baseline_rate[:, None] * rate_dispersion * jitter_amount + jnp.where(surge_events, surge_decay_drops, 0.0)).astype(jnp.float32)


def draw_write_rate(key, part):
    fast_mask, medium_mask = head_classes(key, 0.5)
    key = jax.random.fold_in(key, 37)
    random_child_keys = jax.random.split(key, 4)
    fast_rate = jax.random.uniform(random_child_keys[0], (VALUE_HEADS, PROMPT_TOKENS), minval=0.2, maxval=0.9)
    slow_scale = jnp.exp(jax.random.uniform(random_child_keys[1], (VALUE_HEADS,), minval=-1.6, maxval=0.0)) * D_K / SEGMENT_LONGEST
    jitter_amount = jax.random.uniform(random_child_keys[2], (VALUE_HEADS, PROMPT_TOKENS), minval=0.5, maxval=1.5)
    medium_write = jax.random.uniform(random_child_keys[3], (VALUE_HEADS, PROMPT_TOKENS), minval=0.03, maxval=0.12)
    slow_write = slow_scale[:, None] * jitter_amount
    return jnp.where(fast_mask[:, None], fast_rate, jnp.where(medium_mask[:, None], medium_write, slow_write)).astype(jnp.float32)


def shard_levels(own_key, shape, shards, low, top_value):
    def one(dim, shards_of):
        draws = jax.random.uniform(jax.random.fold_in(jax.random.fold_in(own_key, 6), dim), (shards_of,), jnp.float32, low / len(shards), top_value / len(shards))
        return jnp.repeat(jnp.exp(draws), shape[dim] // shards_of).reshape((-1,) + (1,) * (len(shape) - dim - 1))

    factor_of = one(*shards[0])
    for cut in shards[1:]:
        factor_of = factor_of * one(*cut)
    return factor_of


def length_profile(amount, total, bound, slope):
    weights = [(1 << 20) // math.isqrt(rank ** slope) + 1 for rank in range(2, amount + 1)]
    surplus, holding = total - bound - (amount - 1), [1] * (amount - 1)
    while surplus > 0:
        candidates = [i for i in range(amount - 1) if holding[i] < bound]
        whole, remaining = sum([weights[i] for i in candidates]), surplus
        for i in candidates:
            more = min(bound - holding[i], max(1, remaining * weights[i] // whole), surplus)
            holding[i] = holding[i] + more
            surplus = surplus - more
    return np.array([bound] + holding)


def ragged(key, amount, total, limit, skew):
    if amount == 2:
        one = jax.random.randint(key, (), max(1, total - limit), min(limit, total - 1) + 1)
        return jnp.stack([one, total - one])
    tallies = jnp.asarray(length_profile(amount, total, limit, skew), jnp.int32)
    couples = (amount - 1) // 2
    giver, sink = tallies[1:1 + 2 * couples:2], tallies[2:2 + 2 * couples:2]
    room = jnp.minimum(giver - 1, limit - sink)
    passed = jax.random.randint(jax.random.fold_in(key, 1), (couples,), 0, 1 << 20) % (room + 1)
    tallies = tallies.at[1:1 + 2 * couples:2].set(giver - passed).at[2:2 + 2 * couples:2].set(sink + passed)
    return tallies[jax.random.permutation(jax.random.fold_in(key, 2), amount)]


def bell_draw(key, shape, scale, reach, shards=(), dtype=jnp.bfloat16):
    entries = scale * jax.random.normal(key, shape, jnp.float32)
    if shards:
        entries = entries * shard_levels(key, shape, shards, -0.22, 0.18)
    return jnp.clip(entries, -reach, reach).astype(dtype)


def setup_inputs(seed: int = 0) -> dict:
    key_list = jax.random.split(jax.random.key(seed), 8)
    return {
        "queries": bell_draw(key_list[0], (PROMPT_TOKENS, HK * D_K), 1.0, 6.0, ((0, 32),)),
        "key_vectors": bell_draw(key_list[1], (PROMPT_TOKENS, HK * D_K), 1.0, 6.0, ((0, 32),)),
        "values": bell_draw(key_list[2], (PROMPT_TOKENS, VALUE_HEADS * D_V), 1.0, 6.0, ((0, 32),)),
        "log_decay": draw_log_decay(jax.random.fold_in(key_list[7], 71), 0),
        "write_rate": draw_write_rate(jax.random.fold_in(key_list[7], 71), 0),
        "passage_lengths": ragged(key_list[5], NPASS, PROMPT_TOKENS, SEGMENT_LONGEST, 2).astype(jnp.int32),
        "norm_gain": jnp.clip(1.0 + 0.18 * jax.random.normal(key_list[6], (D_V,), jnp.float32), 0.1, 1.9),
    }


def unit_norm(tensor):
    return tensor * lax.rsqrt(lax.optimization_barrier(jnp.sum(tensor * tensor, axis=-1, keepdims=True)) + 1e-06)

def reference(queries, key_vectors, values, log_decay, write_rate, passage_lengths, norm_gain):
    group_size = VALUE_HEADS // HK
    starts = (jnp.cumsum(passage_lengths) - passage_lengths).astype(jnp.int32)
    resets = jnp.zeros((PROMPT_TOKENS,), jnp.float32).at[starts].set(1.0)
    query_rows = queries.reshape(PROMPT_TOKENS, HK, D_K)
    key_rows = key_vectors.reshape(PROMPT_TOKENS, HK, D_K)
    value_rows = values.reshape(PROMPT_TOKENS, VALUE_HEADS, D_V)
    decay_rows = jnp.transpose(log_decay)
    rate_rows = jnp.transpose(write_rate)

    def advance(carried, inputs):
        query_t, key_t, value_t, decay_t, rate_t, reset_t = inputs
        query_unit = jnp.repeat(unit_norm(query_t.astype(jnp.float32)), group_size, axis=0)
        key_unit = jnp.repeat(unit_norm(key_t.astype(jnp.float32)), group_size, axis=0)
        factor = jnp.exp(decay_t) * (1.0 - reset_t)
        decayed = carried * factor[:, None, None]
        predicted = jnp.einsum('hkd,hk->hd', decayed, key_unit, precision=lax.Precision.HIGHEST)
        written = rate_t[:, None] * (value_t.astype(jnp.float32) - predicted)
        carried = decayed + key_unit[:, :, None] * written[:, None, :]
        output = jnp.einsum('hkd,hk->hd', carried, query_unit, precision=lax.Precision.HIGHEST)
        inverse_rms = lax.rsqrt(lax.optimization_barrier(jnp.mean(output * output, axis=-1, keepdims=True)) + 1e-06)
        return (carried, (output * inverse_rms * norm_gain).astype(jnp.bfloat16))
    initial = jnp.zeros((VALUE_HEADS, D_K, D_V), jnp.float32)
    final_state, outputs = lax.scan(advance, initial, (query_rows, key_rows, value_rows, decay_rows, rate_rows, resets))
    return outputs.reshape(PROMPT_TOKENS, VALUE_HEADS * D_V)
```

```python
import functools

import jax
import jax.numpy as jnp
from jax import lax
from jax.experimental import pallas as pl
from jax.experimental.pallas import tpu as pltpu
from jax.sharding import PartitionSpec as P

D = 128
VALUE_HEADS = 16
HK = 8
BLOCK = 128
AXES = ("seq", "sub")
CHIPS = 4
GROUP = 2 * CHIPS
PHASES = ((0, 1),)
LONGEST = {4096: 2048, 65536: 8192}

f32 = jnp.float32
bf16 = jnp.bfloat16
VMEM = pl.BlockSpec(memory_space=pltpu.VMEM)
SMEM = pl.BlockSpec(memory_space=pltpu.SMEM)


def head_of(core, chip, part):
    return 8 * core + 2 * chip + part


def my_rank(n_sub):
    return lax.axis_index("seq") * n_sub + lax.axis_index("sub")


def mm(a, b):
    return lax.dot_general(a, b, (((1,), (0,)), ((), ())), preferred_element_type=f32)


def mm_nt(a, b, precision=None):
    return lax.dot_general(
        a, b, (((1,), (1,)), ((), ())), preferred_element_type=f32, precision=precision
    )


def split(x):
    high = x.astype(bf16)
    return high, (x - high.astype(f32)).astype(bf16)


def mm3(a, b):
    a_high, a_low = split(a)
    b_high, b_low = split(b)
    return mm(a_high, b_high) + (mm(a_high, b_low) + mm(a_low, b_high))


def mm2(a, b):
    a_high, a_low = split(a)
    return mm(a_high, b) + mm(a_low, b)


def compose(later, early):
    both = mm3(later[:, :D], early)
    return jnp.concatenate([both[:, :D], both[:, D:] + later[:, D:]], axis=1)


def iota(axis):
    return lax.broadcasted_iota(jnp.int32, (BLOCK, BLOCK), axis)


def token_masks(lengths_ref, n_sub):
    first = my_rank(n_sub) * BLOCK
    row_at = first + lax.broadcasted_iota(jnp.int32, (1, BLOCK), 1)
    col_at = first + lax.broadcasted_iota(jnp.int32, (BLOCK, 1), 0)

    def one(i, carried):
        start, row, col, before = carried
        row = row + (row_at >= start).astype(jnp.int32)
        col = col + (col_at >= start).astype(jnp.int32)
        before = before + (first > start).astype(jnp.int32)
        return start + lengths_ref[i], row, col, before

    zero = jnp.int32(0)
    _, row, col, before = lax.fori_loop(
        0,
        lengths_ref.shape[0],
        one,
        (zero, jnp.zeros((1, BLOCK), jnp.int32), jnp.zeros((BLOCK, 1), jnp.int32), zero),
    )
    return row, col, before


def gates(decay_ref, rate_ref):
    decay = decay_ref[...]
    lower = (iota(0) >= iota(1)).astype(f32)
    eye = (iota(0) == iota(1)).astype(f32)
    highest = lax.Precision.HIGHEST
    sum_row = mm_nt(decay, lower, highest)
    sum_col = mm_nt(lower, decay, highest)
    rate_row = rate_ref[...]
    rate_col = mm_nt(eye, rate_row, highest)
    return sum_row, sum_col, rate_row, rate_col


def key_norms(key, key_t):
    wide = key.astype(f32)
    col = lax.rsqrt(jnp.sum(wide * wide, axis=1, keepdims=True) + 1e-06)
    wide_t = key_t.astype(f32)
    row = lax.rsqrt(jnp.sum(wide_t * wide_t, axis=0, keepdims=True) + 1e-06)
    return col, row


def maps_kernel(
    parts, n_sub, lengths_ref, k_ref, v_ref, decay_ref, rate_ref, keep_ref, send_ref, inverse_ref
):
    core = lax.rem(my_rank(n_sub), 2)
    seg_row, seg_col, before = token_masks(lengths_ref, n_sub)
    sum_row, sum_col, rate_row, rate_col = gates(decay_ref, rate_ref)
    apart = iota(0) ^ iota(1)
    strict = (iota(0) > iota(1)) & (seg_row == seg_col)
    eye = (apart == 0).astype(f32)
    reaches = (seg_row == before).astype(f32)
    last = seg_row[:, BLOCK - 1 :]
    ends_col = (seg_col == last).astype(f32)

    for core_of in range(2):
        for chip in range(CHIPS):
            j = 4 * core_of + chip
            key = k_ref[:, j * D : (j + 1) * D]
            key_t = key.T
            n_col, n_row = key_norms(key, key_t)
            gram = mm(key, key_t) * n_row
            for place, part in enumerate(parts):
                h = head_of(core_of, chip, part)
                s_row, s_col = sum_row[h : h + 1, :], sum_col[:, h : h + 1]
                b_row, b_col = rate_row[h : h + 1, :], rate_col[:, h : h + 1]
                between = jnp.exp(jnp.minimum(s_col - s_row, 0.0))
                system = jnp.where(strict, between * gram * (b_col * n_col), 0.0)
                solved = eye - jnp.where(apart == 1, system, 0.0)
                size = 2
                while size < BLOCK:
                    corner = jnp.where((apart >= size) & (apart < 2 * size), system, 0.0)
                    solved = solved - mm3(solved, mm3(corner, solved))
                    size = 2 * size
                inverse_ref[h // 2, place] = solved
                from_row = jnp.exp(s_row) * reaches
                to_end = jnp.exp(s_col[BLOCK - 1 :, :] - s_col) * ends_col
                value = v_ref[:, h * D : (h + 1) * D]
                fresh = mm2(solved * b_row, value)
                wy = mm2(solved * (b_row * from_row * n_row), key)
                scaled = jnp.concatenate([wy, fresh], axis=1) * (to_end * n_col)
                high, low = split(scaled)
                both = mm(key_t, high) + mm(key_t, low)
                whole = from_row[:, BLOCK - 1 :]
                pair = jnp.concatenate([whole * eye - both[:, :D], both[:, D:]], axis=1)

                @pl.when(core == core_of)
                def _():
                    keep_ref[chip, place] = pair

                @pl.when(core != core_of)
                def _():
                    send_ref[chip, place] = pair


def chip_kernel(n_sub, keep_ref, recv_ref, *out_refs):
    rank = my_rank(n_sub)
    core, chip = lax.rem(rank, 2), lax.rem(rank // 2, CHIPS)
    first = core == 0
    for slot in range(CHIPS):
        other = chip ^ slot
        for place in range(keep_ref.shape[1]):
            mine, theirs = keep_ref[other, place], recv_ref[other, place]
            early = jnp.where(first, mine, theirs)
            late = jnp.where(first, theirs, mine)
            out_refs[slot][place] = compose(late, early)


def group_kernel(n_sub, r0, r1, r2, r3, total_map_ref, total_add_ref, ahead_ref, held):
    rank = my_rank(n_sub)
    chip = lax.rem(rank // 2, CHIPS)
    for slot, ref in enumerate((r0, r1, r2, r3)):
        held[chip ^ slot] = ref[...]
    for place in range(r0.shape[0]):
        one = held[0, place]
        two = compose(held[1, place], one)
        upper = compose(held[3, place], held[2, place])
        total = compose(upper, two)
        total_map_ref[place] = total[:, :D]
        total_add_ref[place] = total[:, D:]
        ahead_ref[place, 0] = one
        ahead_ref[place, 1] = two
        ahead_ref[place, 2] = compose(held[2, place], two)


def step_kernel(map_ref, add_ref, state_ref, out_ref):
    for place in range(map_ref.shape[0]):
        out_ref[place] = add_ref[place] + mm3(map_ref[place], state_ref[place])


def spread_kernel(n_sub, ahead_ref, state_ref, o0, o1, o2, o3, held):
    rank = my_rank(n_sub)
    chip = lax.rem(rank // 2, CHIPS)
    for place in range(state_ref.shape[0]):
        state = state_ref[place]
        held[0, place] = state
        for i in range(CHIPS - 1):
            held[i + 1, place] = (
                mm3(ahead_ref[place, i, :, :D], state) + ahead_ref[place, i, :, D:]
            )
    for slot, ref in enumerate((o0, o1, o2, o3)):
        ref[...] = held[chip ^ slot]


def readout_kernel(
    n_sub,
    n_phases,
    lengths_ref,
    q_ref,
    k_ref,
    v_ref,
    decay_ref,
    rate_ref,
    *refs,
):
    inverse_refs = refs[:n_phases]
    recv_refs = refs[n_phases : 2 * n_phases]
    extra_refs = refs[2 * n_phases : 3 * n_phases]
    read_ref = refs[3 * n_phases]
    core = lax.rem(my_rank(n_sub), 2)
    seg_row, seg_col, before = token_masks(lengths_ref, n_sub)
    sum_row, sum_col, rate_row, rate_col = gates(decay_ref, rate_ref)
    lower = (iota(0) >= iota(1)) & (seg_row == seg_col)
    reaches_row = (seg_row == before).astype(f32)
    reaches_col = (seg_col == before).astype(f32)
    per_phase = 2 // n_phases
    for j in range(HK):
        key = k_ref[:, j * D : (j + 1) * D]
        key_t = key.T
        n_col, n_row = key_norms(key, key_t)
        query = q_ref[:, j * D : (j + 1) * D]
        wide = query.astype(f32)
        q_col = lax.rsqrt(jnp.sum(wide * wide, axis=1, keepdims=True) + 1e-06)
        cross = mm(query, key_t) * n_row
        for part in range(2):
            h = 2 * j + part
            phase, place = part // per_phase, part % per_phase
            s_row, s_col = sum_row[h : h + 1, :], sum_col[:, h : h + 1]
            b_row = rate_row[h : h + 1, :]
            between = jnp.exp(jnp.minimum(s_col - s_row, 0.0))
            scores = jnp.where(lower, between * cross * q_col, 0.0)
            mixed = mm3(scores, inverse_refs[phase][j, place])
            from_row = jnp.exp(s_row) * reaches_row
            from_col = jnp.exp(s_col) * reaches_col
            fresh = mm2(mixed * b_row, v_ref[:, h * D : (h + 1) * D])
            through = wide * (from_col * q_col) - mm2(mixed * (b_row * from_row * n_row), key)

            @pl.when(core == 0)
            def _():
                read_ref[h] = jnp.concatenate([through, fresh], axis=1)

            @pl.when(core == 1)
            def _():
                source = recv_refs[phase] if j >= 4 else extra_refs[phase]
                both = mm3(through, source[j % 4, place])
                read_ref[h] = jnp.concatenate([both[:, :D], both[:, D:] + fresh], axis=1)


def output_kernel(n_sub, n_phases, gain_ref, read_ref, *refs):
    out_ref = refs[-1]
    rank = my_rank(n_sub)
    core, chip = lax.rem(rank, 2), lax.rem(rank // 2, CHIPS)
    per_phase = 2 // n_phases
    gain = gain_ref[...]
    for phase in range(n_phases):
        for swapped in range(2):
            for slot in range(CHIPS):
                states = refs[(phase * 2 + swapped) * CHIPS + slot]
                for place in range(per_phase):
                    h = head_of(core ^ swapped, chip ^ slot, phase * per_phase + place)
                    read = read_ref[h]
                    raw = mm3(read[:, :D], states[place]) + read[:, D:]
                    scale = lax.rsqrt(jnp.mean(raw * raw, axis=1, keepdims=True) + 1e-06)
                    at = pl.multiple_of(h * D, D)
                    out_ref[:, pl.ds(at, D)] = (raw * scale * gain).astype(bf16)


def call(kernel, outs, args, scratch=(), specs=None, flops=0, name=None):
    moved = sum(a.size * a.dtype.itemsize for a in args)
    moved += sum(o.size * o.dtype.itemsize for o in jax.tree.leaves(outs))
    return pl.pallas_call(
        kernel,
        out_shape=outs,
        in_specs=[VMEM] * len(args) if specs is None else specs,
        out_specs=jax.tree.map(lambda o: VMEM, outs),
        scratch_shapes=list(scratch),
        compiler_params=pltpu.CompilerParams(vmem_limit_bytes=32 * 2**20),
        cost_estimate=pl.CostEstimate(flops=flops, bytes_accessed=moved, transcendentals=0),
        name=name,
    )(*args)


def like(*shape):
    return jax.ShapeDtypeStruct(shape, f32)


def on_device(
    n_dev,
    n_sub,
    queries,
    key_vectors,
    values,
    log_decay,
    write_rate,
    passage_lengths,
    norm_gain,
):
    assert values.shape[0] == BLOCK
    tokens = n_dev * BLOCK
    longest = LONGEST.get(tokens, tokens)
    reach = min(-(-longest // (GROUP * BLOCK)), n_dev // GROUP)
    n_phases = len(PHASES)
    n = 2 // n_phases
    swap_pairs = [(i, i ^ 1) for i in range(n_dev)]
    up_pairs = [(i, i + 1) for i in range(0, n_dev, 2)]
    next_pairs = [(i, i + GROUP) for i in range(n_dev - GROUP)]

    def chip_pairs(slot):
        return [(i, i ^ (2 * slot)) for i in range(n_dev)]

    def permute(x, pairs):
        return lax.ppermute(x, AXES, pairs)

    step = 2 * BLOCK**3
    inverses, recvs, extras, states = [], [], [], []
    for parts in PHASES:
        keep, send, inverse = call(
            functools.partial(maps_kernel, parts, n_sub),
            (like(CHIPS, n, D, 2 * D), like(CHIPS, n, D, 2 * D), like(HK, n, BLOCK, BLOCK)),
            (passage_lengths, key_vectors, values, log_decay, write_rate),
            specs=[SMEM, VMEM, VMEM, VMEM, VMEM],
            flops=8 * n * 44 * step,
            name="maps",
        )
        recv = permute(send, swap_pairs)
        extra = permute(keep, up_pairs)
        inverses.append(inverse)
        recvs.append(recv)
        extras.append(extra)
        slots = call(
            functools.partial(chip_kernel, n_sub),
            (like(n, D, 2 * D),) * CHIPS,
            (keep, recv),
            flops=4 * n * 6 * step,
            name="chip",
        )
        got = [slots[0]] + [permute(slots[s], chip_pairs(s)) for s in range(1, CHIPS)]
        total_map, total_add, ahead = call(
            functools.partial(group_kernel, n_sub),
            (like(n, D, D), like(n, D, D), like(n, 3, D, 2 * D)),
            got,
            scratch=(pltpu.VMEM((CHIPS, n, D, 2 * D), f32),),
            flops=n * 24 * step,
            name="group",
        )
        state = total_add
        for _ in range(reach - 1):
            state = permute(state, next_pairs)
            state = call(
                step_kernel,
                like(n, D, D),
                (total_map, total_add, state),
                flops=n * 3 * step,
                name="step",
            )
        state = permute(state, next_pairs)
        outs = call(
            functools.partial(spread_kernel, n_sub),
            (like(n, D, D),) * CHIPS,
            (ahead, state),
            scratch=(pltpu.VMEM((CHIPS, n, D, D), f32),),
            flops=n * 9 * step,
            name="spread",
        )
        own = [outs[0]] + [permute(outs[s], chip_pairs(s)) for s in range(1, CHIPS)]
        states += own + [permute(x, swap_pairs) for x in own]

    read = call(
        functools.partial(readout_kernel, n_sub, n_phases),
        like(VALUE_HEADS, BLOCK, 2 * D),
        (
            passage_lengths,
            queries,
            key_vectors,
            values,
            log_decay,
            write_rate,
            *inverses,
            *recvs,
            *extras,
        ),
        specs=[SMEM] + [VMEM] * (5 + 3 * n_phases),
        flops=16 * 13 * step,
        name="readout",
    )
    return call(
        functools.partial(output_kernel, n_sub, n_phases),
        jax.ShapeDtypeStruct((BLOCK, VALUE_HEADS * D), bf16),
        (norm_gain.reshape(1, D), read, *states),
        flops=16 * 3 * step,
        name="output",
    )


def solution(mesh):
    n_sub = mesh.shape["sub"]
    n_dev = mesh.shape["seq"] * n_sub
    tokens = P(AXES, None)
    heads = P(None, AXES)
    return jax.shard_map(
        functools.partial(on_device, n_dev, n_sub),
        mesh=mesh,
        in_specs=(tokens, tokens, tokens, heads, heads, P(), P()),
        out_specs=tokens,
        check_vma=False,
    )
```

```python
import functools

import jax
import jax.numpy as jnp
from jax import lax
from jax.experimental import pallas as pl
from jax.experimental.pallas import tpu as pltpu
from jax.sharding import PartitionSpec as P

D = 128
VALUE_HEADS = 16
HK = 8
BLOCK = 128
AXES = ("seq", "sub")
CHIPS = 4
GROUP = 2 * CHIPS
PHASES = ((0, 1),)
LONGEST = {4096: 2048, 65536: 8192}

f32 = jnp.float32
bf16 = jnp.bfloat16
VMEM = pl.BlockSpec(memory_space=pltpu.VMEM)
ANY = pl.BlockSpec(memory_space=pl.ANY)
SMEM = pl.BlockSpec(memory_space=pltpu.SMEM)


def head_of(core, chip, part):
    return 8 * core + 2 * chip + part


def my_rank(n_sub):
    return lax.axis_index("seq") * n_sub + lax.axis_index("sub")


def mm(a, b):
    return lax.dot_general(a, b, (((1,), (0,)), ((), ())), preferred_element_type=f32)


def mm_nt(a, b, precision=None):
    return lax.dot_general(
        a, b, (((1,), (1,)), ((), ())), preferred_element_type=f32, precision=precision
    )


def split(x):
    high = x.astype(bf16)
    return high, (x - high.astype(f32)).astype(bf16)


def left(x):
    return jnp.concatenate(split(x), axis=1)


def right(x):
    wide = jnp.concatenate(split(x), axis=1)
    return jnp.concatenate([wide, wide], axis=0)


def fold(x):
    half = x.shape[1] // 2
    return x[:, :half] + x[:, half:]


def mm3(a, b):
    return fold(mm(left(a), right(b)))


def mm2(a, b):
    return mm(left(a), twice(b))


def twice(x):
    return jnp.concatenate([x, x], axis=0)


def compose(later, early):
    both = mm3(later[:, :D], early)
    return jnp.concatenate([both[:, :D], both[:, D:] + later[:, D:]], axis=1)


def iota(axis):
    return lax.broadcasted_iota(jnp.int32, (BLOCK, BLOCK), axis)


def token_masks(lengths_ref, n_sub):
    first = my_rank(n_sub) * BLOCK
    row_at = first + lax.broadcasted_iota(jnp.int32, (1, BLOCK), 1)
    col_at = first + lax.broadcasted_iota(jnp.int32, (BLOCK, 1), 0)

    def one(i, carried):
        start, row, col, before = carried
        row = row + (row_at >= start).astype(jnp.int32)
        col = col + (col_at >= start).astype(jnp.int32)
        before = before + (first > start).astype(jnp.int32)
        return start + lengths_ref[i], row, col, before

    zero = jnp.int32(0)
    _, row, col, before = lax.fori_loop(
        0,
        lengths_ref.shape[0],
        one,
        (zero, jnp.zeros((1, BLOCK), jnp.int32), jnp.zeros((BLOCK, 1), jnp.int32), zero),
    )
    return row, col, before


def gates(decay_ref, rate_ref):
    decay = decay_ref[...]
    lower = (iota(0) >= iota(1)).astype(f32)
    eye = (iota(0) == iota(1)).astype(f32)
    highest = lax.Precision.HIGHEST
    sum_row = mm_nt(decay, lower, highest)
    sum_col = mm_nt(lower, decay, highest)
    rate_row = rate_ref[...]
    rate_col = mm_nt(eye, rate_row, highest)
    return sum_row, sum_col, rate_row, rate_col


def key_norms(key, key_t):
    wide = key.astype(f32)
    col = lax.rsqrt(jnp.sum(wide * wide, axis=1, keepdims=True) + 1e-06)
    wide_t = key_t.astype(f32)
    row = lax.rsqrt(jnp.sum(wide_t * wide_t, axis=0, keepdims=True) + 1e-06)
    return col, row


def fetch(pairs, sems):
    copies = [pltpu.make_async_copy(a, b, sems.at[i]) for i, (a, b) in enumerate(pairs)]
    for copy in copies:
        copy.start()
    for copy in copies:
        copy.wait()


def odd_rows(x, size):
    return jnp.concatenate([x[i : i + size] for i in range(size, BLOCK, 2 * size)], axis=0)


def with_odd_rows(x, rows, size):
    pieces = []
    for i in range(0, BLOCK // 2, size):
        pieces += [x[2 * i : 2 * i + size], rows[i : i + size]]
    return jnp.concatenate(pieces, axis=0)


def invert(systems, apart):
    eye = (apart == 0).astype(f32)
    near = apart < 16
    powers = [jnp.where(near, n, 0.0) for n in systems]
    solved = [eye - n for n in powers]
    powers = [mm3(n, n) for n in powers]
    for last in (False, False, True):
        rights = [right(n) for n in powers]
        if last:
            solved = [s + fold(mm(left(s), r)) for s, r in zip(solved, rights)]
        else:
            both = [
                fold(mm(left(jnp.concatenate([n, s], axis=0)), r))
                for n, s, r in zip(powers, solved, rights)
            ]
            powers = [x[:BLOCK] for x in both]
            solved = [s + x[BLOCK:] for s, x in zip(solved, both)]
    size = 16
    while size < BLOCK:
        band = odd_rows((apart >= size) & (apart < 2 * size), size)
        corners = [jnp.where(band, odd_rows(n, size), 0.0) for n in systems]
        products = [mm3(c, s) for c, s in zip(corners, solved)]
        zero = jnp.zeros((BLOCK, BLOCK), f32)
        fulls = [with_odd_rows(zero, p, size) for p in products]
        rows = [odd_rows(s, size) for s in solved]
        rows = [r - mm3(r, u) for r, u in zip(rows, fulls)]
        solved = [with_odd_rows(s, r, size) for s, r in zip(solved, rows)]
        size = 2 * size
    return solved


def maps_kernel(
    parts,
    n_sub,
    lengths_hbm,
    k_hbm,
    v_hbm,
    decay_hbm,
    rate_hbm,
    keep_ref,
    send_ref,
    inverse_ref,
    lengths_ref,
    k_ref,
    v_ref,
    decay_ref,
    rate_ref,
    middle,
    weights,
    wholes,
    sems,
):
    fetch(
        (
            (lengths_hbm, lengths_ref),
            (k_hbm, k_ref),
            (decay_hbm, decay_ref),
            (rate_hbm, rate_ref),
            (v_hbm, v_ref),
        ),
        sems,
    )
    core = lax.rem(my_rank(n_sub), 2)
    seg_row, seg_col, before = token_masks(lengths_ref, n_sub)
    sum_row, sum_col, rate_row, rate_col = gates(decay_ref, rate_ref)
    apart = iota(0) ^ iota(1)
    strict = (iota(0) > iota(1)) & (seg_row == seg_col)
    eye = (apart == 0).astype(f32)
    reaches = (seg_row == before).astype(f32)
    last = seg_row[:, BLOCK - 1 :]
    ends_col = (seg_col == last).astype(f32)

    n = len(parts)
    batch = 4
    for j0 in range(0, HK, batch // n):
        systems, ends = [], []
        for j in range(j0, j0 + batch // n):
            key = k_ref[:, j * D : (j + 1) * D]
            key_t = key.T
            n_col, n_row = key_norms(key, key_t)
            gram = mm(key, key_t) * n_row
            for place, part in enumerate(parts):
                h = 2 * j + part
                s_row, s_col = sum_row[h : h + 1, :], sum_col[:, h : h + 1]
                b_row, b_col = rate_row[h : h + 1, :], rate_col[:, h : h + 1]
                between = jnp.exp(jnp.minimum(s_col - s_row, 0.0))
                systems.append(jnp.where(strict, between * gram * (b_col * n_col), 0.0))
                from_row = jnp.exp(s_row) * reaches
                ends.append(jnp.exp(s_col[BLOCK - 1 :, :] - s_col) * ends_col * n_col)
                weights[n * j + place, 0:1] = b_row * from_row * n_row
                weights[n * j + place, 1:2] = b_row
                wholes[n * j + place] = from_row[:, BLOCK - 1 :] * eye
        solved = invert(systems, apart)
        for i, (inverse, end) in enumerate(zip(solved, ends)):
            inverse_ref[j0 + i // n, i % n] = inverse
            middle[n * j0 + i] = inverse * end

    for out_ref, core_of in ((send_ref, 1 - core), (keep_ref, core)):
        for chip in range(CHIPS):
            j = CHIPS * core_of + chip
            key = k_ref[:, pl.ds(pl.multiple_of(j * D, D), D)]
            key_t = key.T
            keys, key_ts = twice(key), jnp.concatenate([key_t, key_t], axis=1)
            for place, part in enumerate(parts):
                at = n * j + place
                mid = middle[at]
                value = v_ref[:, pl.ds(pl.multiple_of((2 * j + part) * D, D), D)]
                wy = mm(left(mid * weights[at, 0:1]), keys)
                fresh = mm(left(mid * weights[at, 1:2]), twice(value))
                high, low = split(jnp.concatenate([wy, fresh], axis=1))
                both = mm(key_ts, jnp.concatenate([high, low], axis=0))
                out_ref[chip, place, :, :D] = wholes[at] - both[:, :D]
                out_ref[chip, place, :, D:] = both[:, D:]


def chip_kernel(n_sub, keep_ref, recv_ref, *out_refs):
    rank = my_rank(n_sub)
    core, chip = lax.rem(rank, 2), lax.rem(rank // 2, CHIPS)
    first = core == 0
    for slot in range(CHIPS):
        other = chip ^ slot
        for place in range(keep_ref.shape[1]):
            mine, theirs = keep_ref[other, place], recv_ref[other, place]
            early = jnp.where(first, mine, theirs)
            late = jnp.where(first, theirs, mine)
            out_refs[slot][place] = compose(late, early)


def group_kernel(n_sub, r0, r1, r2, r3, after_ref, total_map_ref, total_add_ref, ahead_ref, held):
    rank = my_rank(n_sub)
    chip = lax.rem(rank // 2, CHIPS)
    for slot, ref in enumerate((r0, r1, r2, r3)):
        held[chip ^ slot] = ref[...]
    for place in range(r0.shape[0]):
        one = held[0, place]
        two = compose(held[1, place], one)
        upper = compose(held[3, place], held[2, place])
        total = compose(upper, two)
        total_map_ref[place] = total[:, :D]
        total_add_ref[place] = total[:, D:]
        ahead_ref[place, 0] = one
        ahead_ref[place, 1] = two
        ahead_ref[place, 2] = compose(held[2, place], two)


def step_kernel(map_ref, add_ref, state_ref, out_ref):
    for place in range(map_ref.shape[0]):
        out_ref[place] = add_ref[place] + mm3(map_ref[place], state_ref[place])


def spread_kernel(n_sub, ahead_ref, state_ref, o0, o1, o2, o3, held):
    rank = my_rank(n_sub)
    chip = lax.rem(rank // 2, CHIPS)
    for place in range(state_ref.shape[0]):
        state = state_ref[place]
        held[0, place] = state
        for i in range(CHIPS - 1):
            held[i + 1, place] = (
                mm3(ahead_ref[place, i, :, :D], state) + ahead_ref[place, i, :, D:]
            )
    for slot, ref in enumerate((o0, o1, o2, o3)):
        ref[...] = held[chip ^ slot]


def readout_kernel(
    n_sub,
    n_phases,
    lengths_ref,
    q_ref,
    k_ref,
    v_ref,
    decay_ref,
    rate_ref,
    *refs,
):
    inverse_refs = refs[:n_phases]
    recv_refs = refs[n_phases : 2 * n_phases]
    extra_refs = refs[2 * n_phases : 3 * n_phases]
    read_ref = refs[3 * n_phases]
    core = lax.rem(my_rank(n_sub), 2)
    seg_row, seg_col, before = token_masks(lengths_ref, n_sub)
    sum_row, sum_col, rate_row, rate_col = gates(decay_ref, rate_ref)
    lower = (iota(0) >= iota(1)) & (seg_row == seg_col)
    reaches_row = (seg_row == before).astype(f32)
    reaches_col = (seg_col == before).astype(f32)
    per_phase = 2 // n_phases
    for j in range(HK):
        key = k_ref[:, j * D : (j + 1) * D]
        key_t = key.T
        n_col, n_row = key_norms(key, key_t)
        query = q_ref[:, j * D : (j + 1) * D]
        wide = query.astype(f32)
        q_col = lax.rsqrt(jnp.sum(wide * wide, axis=1, keepdims=True) + 1e-06)
        cross = mm(query, key_t) * n_row
        for part in range(2):
            h = 2 * j + part
            phase, place = part // per_phase, part % per_phase
            s_row, s_col = sum_row[h : h + 1, :], sum_col[:, h : h + 1]
            b_row = rate_row[h : h + 1, :]
            between = jnp.exp(jnp.minimum(s_col - s_row, 0.0))
            scores = jnp.where(lower, between * cross * q_col, 0.0)
            mixed = mm3(scores, inverse_refs[phase][j, place])
            from_row = jnp.exp(s_row) * reaches_row
            from_col = jnp.exp(s_col) * reaches_col
            fresh = mm2(mixed * b_row, v_ref[:, h * D : (h + 1) * D])
            through = wide * (from_col * q_col) - mm2(mixed * (b_row * from_row * n_row), key)

            read_ref[h] = jnp.concatenate([through, fresh], axis=1)

    @pl.when(core == 1)
    def _():
        for h in range(VALUE_HEADS):
            phase, place = (h % 2) // per_phase, (h % 2) % per_phase
            source = recv_refs[phase] if h >= 8 else extra_refs[phase]
            read = read_ref[h]
            both = mm3(read[:, :D], source[(h // 2) % CHIPS, place])
            read_ref[h, :, :D] = both[:, :D]
            read_ref[h, :, D:] = both[:, D:] + read[:, D:]


def output_kernel(n_sub, n_phases, gain_ref, read_ref, *refs):
    out_ref = refs[-1]
    rank = my_rank(n_sub)
    core, chip = lax.rem(rank, 2), lax.rem(rank // 2, CHIPS)
    per_phase = 2 // n_phases
    gain = gain_ref[...]
    for phase in range(n_phases):
        for swapped in range(2):
            for slot in range(CHIPS):
                states = refs[(phase * 2 + swapped) * CHIPS + slot]
                for place in range(per_phase):
                    h = head_of(core ^ swapped, chip ^ slot, phase * per_phase + place)
                    read = read_ref[h]
                    raw = mm3(read[:, :D], states[place]) + read[:, D:]
                    scale = lax.rsqrt(jnp.mean(raw * raw, axis=1, keepdims=True) + 1e-06)
                    at = pl.multiple_of(h * D, D)
                    out_ref[:, pl.ds(at, D)] = (raw * scale * gain).astype(bf16)


def call(kernel, outs, args, scratch=(), specs=None, flops=0, name=None, vmem=32):
    moved = sum(a.size * a.dtype.itemsize for a in args)
    moved += sum(o.size * o.dtype.itemsize for o in jax.tree.leaves(outs))
    return pl.pallas_call(
        kernel,
        out_shape=outs,
        in_specs=[VMEM] * len(args) if specs is None else specs,
        out_specs=jax.tree.map(lambda o: VMEM, outs),
        scratch_shapes=list(scratch),
        compiler_params=pltpu.CompilerParams(vmem_limit_bytes=vmem * 2**20),
        cost_estimate=pl.CostEstimate(flops=flops, bytes_accessed=moved, transcendentals=0),
        name=name,
    )(*args)


def like(*shape):
    return jax.ShapeDtypeStruct(shape, f32)


def on_device(
    n_dev,
    n_sub,
    queries,
    key_vectors,
    values,
    log_decay,
    write_rate,
    passage_lengths,
    norm_gain,
):
    assert values.shape[0] == BLOCK
    tokens = n_dev * BLOCK
    longest = LONGEST.get(tokens, tokens)
    reach = min(-(-longest // (GROUP * BLOCK)), n_dev // GROUP)
    n_phases = len(PHASES)
    n = 2 // n_phases
    swap_pairs = [(i, i ^ 1) for i in range(n_dev)]
    up_pairs = [(i, i + 1) for i in range(0, n_dev, 2)]
    next_pairs = [(i, i + GROUP) for i in range(n_dev - GROUP)]

    def chip_pairs(slot):
        return [(i, i ^ (2 * slot)) for i in range(n_dev)]

    def permute(x, pairs):
        return lax.ppermute(x, AXES, pairs)

    step = 2 * BLOCK**3
    inverses, recvs, extras, states = [], [], [], []
    for parts in PHASES:
        keep, send, inverse = call(
            functools.partial(maps_kernel, parts, n_sub),
            (like(CHIPS, n, D, 2 * D), like(CHIPS, n, D, 2 * D), like(HK, n, BLOCK, BLOCK)),
            (passage_lengths, key_vectors, values, log_decay, write_rate),
            scratch=(
                pltpu.SMEM(passage_lengths.shape, jnp.int32),
                pltpu.VMEM(key_vectors.shape, bf16),
                pltpu.VMEM(values.shape, bf16),
                pltpu.VMEM(log_decay.shape, f32),
                pltpu.VMEM(write_rate.shape, f32),
                pltpu.VMEM((HK * n, BLOCK, BLOCK), f32),
                pltpu.VMEM((HK * n, 8, BLOCK), f32),
                pltpu.VMEM((HK * n, D, D), f32),
                pltpu.SemaphoreType.DMA((5,)),
            ),
            specs=[ANY] * 5,
            flops=8 * n * 44 * step,
            name="maps",
            vmem=60,
        )
        recv = permute(send, swap_pairs)
        extra = permute(keep, up_pairs)
        inverses.append(inverse)
        recvs.append(recv)
        extras.append(extra)
        slots = call(
            functools.partial(chip_kernel, n_sub),
            (like(n, D, 2 * D),) * CHIPS,
            (keep, recv),
            flops=4 * n * 6 * step,
            name="chip",
        )
        got = [slots[0]] + [permute(slots[s], chip_pairs(s)) for s in range(1, CHIPS)]
        read = call(
            functools.partial(readout_kernel, n_sub, n_phases),
            like(VALUE_HEADS, BLOCK, 2 * D),
            (
                passage_lengths,
                queries,
                key_vectors,
                values,
                log_decay,
                write_rate,
                *inverses,
                *recvs,
                *extras,
            ),
            specs=[SMEM] + [VMEM] * (5 + 3 * n_phases),
            flops=16 * 13 * step,
            name="readout",
        )
        total_map, total_add, ahead = call(
            functools.partial(group_kernel, n_sub),
            (like(n, D, D), like(n, D, D), like(n, 3, D, 2 * D)),
            (*got, read),
            specs=[VMEM] * CHIPS + [ANY],
            scratch=(pltpu.VMEM((CHIPS, n, D, 2 * D), f32),),
            flops=n * 24 * step,
            name="group",
        )
        state = total_add
        for _ in range(reach - 1):
            state = permute(state, next_pairs)
            state = call(
                step_kernel,
                like(n, D, D),
                (total_map, total_add, state),
                flops=n * 3 * step,
                name="step",
            )
        state = permute(state, next_pairs)
        outs = call(
            functools.partial(spread_kernel, n_sub),
            (like(n, D, D),) * CHIPS,
            (ahead, state),
            scratch=(pltpu.VMEM((CHIPS, n, D, D), f32),),
            flops=n * 9 * step,
            name="spread",
        )
        own = [outs[0]] + [permute(outs[s], chip_pairs(s)) for s in range(1, CHIPS)]
        states += own + [permute(x, swap_pairs) for x in own]

    return call(
        functools.partial(output_kernel, n_sub, n_phases),
        jax.ShapeDtypeStruct((BLOCK, VALUE_HEADS * D), bf16),
        (norm_gain.reshape(1, D), read, *states),
        flops=16 * 3 * step,
        name="output",
    )


def solution(mesh):
    n_sub = mesh.shape["sub"]
    n_dev = mesh.shape["seq"] * n_sub
    tokens = P(AXES, None)
    heads = P(None, AXES)
    return jax.shard_map(
        functools.partial(on_device, n_dev, n_sub),
        mesh=mesh,
        in_specs=(tokens, tokens, tokens, heads, heads, P(), P()),
        out_specs=tokens,
        check_vma=False,
    )
```

```python
import functools
import math

import jax
import jax.numpy as jnp
from jax import lax
from jax.experimental import pallas as pl
from jax.experimental.pallas import tpu as pltpu
from jax.sharding import PartitionSpec as P

D = 128
VALUE_HEADS = 16
HK = 8
BLOCK = 128
AXES = ("seq", "sub")
CHIPS = 4
GROUP = 2 * CHIPS
SIDES = (0, 1)
PHASES = ((0, 1, 2, 3),)
BATCH = 8
LONGEST = {4096: 2048, 65536: 8192}

f32 = jnp.float32
bf16 = jnp.bfloat16
VMEM = pl.BlockSpec(memory_space=pltpu.VMEM)
ANY = pl.BlockSpec(memory_space=pl.ANY)
HBM = pl.BlockSpec(memory_space=pltpu.HBM)
SMEM = pl.BlockSpec(memory_space=pltpu.SMEM)


def my_rank(n_sub):
    return lax.axis_index("seq") * n_sub + lax.axis_index("sub")


def mm(a, b):
    return lax.dot_general(a, b, (((1,), (0,)), ((), ())), preferred_element_type=f32)


def mm_nt(a, b, precision=None):
    return lax.dot_general(
        a, b, (((1,), (1,)), ((), ())), preferred_element_type=f32, precision=precision
    )


def split(x):
    high = x.astype(bf16)
    return high, (x - high.astype(f32)).astype(bf16)


def left(x):
    return jnp.concatenate(split(x), axis=1)


def right(x):
    wide = jnp.concatenate(split(x), axis=1)
    return jnp.concatenate([wide, wide], axis=0)


def fold(x):
    half = x.shape[1] // 2
    return x[:, :half] + x[:, half:]


def mm3(a, b):
    return fold(mm(left(a), right(b)))


def mm2(a, b):
    return mm(left(a), twice(b))


def twice(x):
    return jnp.concatenate([x, x], axis=0)


def compose(later, early):
    both = mm3(later[:, :D], early)
    return jnp.concatenate([both[:, :D], both[:, D:] + later[:, D:]], axis=1)


def iota(axis):
    return lax.broadcasted_iota(jnp.int32, (BLOCK, BLOCK), axis)


def token_masks(lengths_ref, n_sub):
    first = my_rank(n_sub) * BLOCK
    row_at = first + lax.broadcasted_iota(jnp.int32, (1, BLOCK), 1)
    col_at = first + lax.broadcasted_iota(jnp.int32, (BLOCK, 1), 0)

    def one(i, carried):
        start, row, col, before = carried
        row = row + (row_at >= start).astype(jnp.int32)
        col = col + (col_at >= start).astype(jnp.int32)
        before = before + (first > start).astype(jnp.int32)
        return start + lengths_ref[i], row, col, before

    zero = jnp.int32(0)
    _, row, col, before = lax.fori_loop(
        0,
        lengths_ref.shape[0],
        one,
        (zero, jnp.zeros((1, BLOCK), jnp.int32), jnp.zeros((BLOCK, 1), jnp.int32), zero),
    )
    return row, col, before


def gates(heads, decay_ref, rate_ref):
    decay = jnp.concatenate([decay_ref[pl.ds(h, 1), :] for h in heads], axis=0)
    rate_row = jnp.concatenate([rate_ref[pl.ds(h, 1), :] for h in heads], axis=0)
    lower = (iota(0) >= iota(1)).astype(f32)
    eye = (iota(0) == iota(1)).astype(f32)
    highest = lax.Precision.HIGHEST
    sum_row = mm_nt(decay, lower, highest)
    sum_col = mm_nt(lower, decay, highest)
    rate_col = mm_nt(eye, rate_row, highest)
    return sum_row, sum_col, rate_row, rate_col


def columns(ref, at):
    return ref[:, pl.ds(pl.multiple_of(at * D, D), D)]


def key_heads(n_sub, slots):
    rank = my_rank(n_sub)
    core, chip = lax.rem(rank, 2), lax.rem(rank // 2, CHIPS)
    return [CHIPS * (core ^ side) + (chip ^ slot) for side in SIDES for slot in slots]


def value_heads(keys):
    return [2 * j + part for j in keys for part in range(2)]


def key_norms(key, key_t):
    wide = key.astype(f32)
    col = lax.rsqrt(jnp.sum(wide * wide, axis=1, keepdims=True) + 1e-06)
    wide_t = key_t.astype(f32)
    row = lax.rsqrt(jnp.sum(wide_t * wide_t, axis=0, keepdims=True) + 1e-06)
    return col, row


def fetch(pairs, sems):
    copies = [pltpu.make_async_copy(a, b, sems.at[i]) for i, (a, b) in enumerate(pairs)]
    for copy in copies:
        copy.start()
    for copy in copies:
        copy.wait()


def odd_rows(x, size):
    return jnp.concatenate([x[i : i + size] for i in range(size, BLOCK, 2 * size)], axis=0)


def with_odd_rows(x, rows, size):
    pieces = []
    for i in range(0, BLOCK // 2, size):
        pieces += [x[2 * i : 2 * i + size], rows[i : i + size]]
    return jnp.concatenate(pieces, axis=0)


def invert(systems, apart):
    eye = (apart == 0).astype(f32)
    near = apart < 16
    powers = [jnp.where(near, n, 0.0) for n in systems]
    solved = [eye - n for n in powers]
    powers = [mm3(n, n) for n in powers]
    for last in (False, False, True):
        rights = [right(n) for n in powers]
        if last:
            solved = [s + fold(mm(left(s), r)) for s, r in zip(solved, rights)]
        else:
            both = [
                fold(mm(left(jnp.concatenate([n, s], axis=0)), r))
                for n, s, r in zip(powers, solved, rights)
            ]
            powers = [x[:BLOCK] for x in both]
            solved = [s + x[BLOCK:] for s, x in zip(solved, both)]
    size = 16
    while size < BLOCK:
        band = odd_rows((apart >= size) & (apart < 2 * size), size)
        corners = [jnp.where(band, odd_rows(n, size), 0.0) for n in systems]
        products = [mm3(c, s) for c, s in zip(corners, solved)]
        zero = jnp.zeros((BLOCK, BLOCK), f32)
        fulls = [with_odd_rows(zero, p, size) for p in products]
        rows = [odd_rows(s, size) for s in solved]
        rows = [r - mm3(r, u) for r, u in zip(rows, fulls)]
        solved = [with_odd_rows(s, r, size) for s, r in zip(solved, rows)]
        size = 2 * size
    return solved


def maps_kernel(slots, n_sub, *refs):
    if len(refs) == 9:
        keep_ref, send_ref, inverse_ref = refs[6:]
    else:
        keep_ref, send_ref, inverse_ref = refs[5:8]
        fetch(list(zip(refs[:5], refs[8:13])), refs[13])
        refs = refs[8:]
    lengths_ref, k_ref, v_ref, decay_ref, rate_ref = refs[:5]
    keys = key_heads(n_sub, slots)
    heads = value_heads(keys)
    seg_row, seg_col, before = token_masks(lengths_ref, n_sub)
    sum_row, sum_col, rate_row, rate_col = gates(heads, decay_ref, rate_ref)
    apart = iota(0) ^ iota(1)
    strict = (iota(0) > iota(1)) & (seg_row == seg_col)
    eye = (apart == 0).astype(f32)
    reaches = (seg_row == before).astype(f32)
    last = seg_row[:, BLOCK - 1 :]
    ends_col = (seg_col == last).astype(f32)

    for j0 in range(0, len(keys), BATCH // 2):
        systems, details = [], []
        for j in range(j0, j0 + BATCH // 2):
            key = columns(k_ref, keys[j])
            key_t = key.T
            n_col, n_row = key_norms(key, key_t)
            gram = mm(key, key_t) * n_row
            for part in range(2):
                i = 2 * j + part
                s_row, s_col = sum_row[i : i + 1, :], sum_col[:, i : i + 1]
                b_row, b_col = rate_row[i : i + 1, :], rate_col[:, i : i + 1]
                between = jnp.exp(jnp.minimum(s_col - s_row, 0.0))
                systems.append(jnp.where(strict, between * gram * (b_col * n_col), 0.0))
                from_row = jnp.exp(s_row) * reaches
                end = jnp.exp(s_col[BLOCK - 1 :, :] - s_col) * ends_col * n_col
                details.append((i, key, key_t, n_row, b_row, from_row, end))
        solved = invert(systems, apart)
        for inverse, (i, key, key_t, n_row, b_row, from_row, end) in zip(solved, details):
            inverse_ref[i] = inverse
            middle = inverse * end
            wy = mm(left(middle * (b_row * from_row * n_row)), twice(key))
            fresh = mm(left(middle * b_row), twice(columns(v_ref, heads[i])))
            high, low = split(jnp.concatenate([wy, fresh], axis=1))
            key_ts = jnp.concatenate([key_t, key_t], axis=1)
            both = mm(key_ts, jnp.concatenate([high, low], axis=0))
            out_ref = keep_ref if i < len(heads) // 2 else send_ref
            at = i % (len(heads) // 2)
            out_ref[at, :, :D] = from_row[:, BLOCK - 1 :] * eye - both[:, :D]
            out_ref[at, :, D:] = both[:, D:]


def chip_kernel(n_sub, keep_ref, recv_ref, *out_refs):
    first = lax.rem(my_rank(n_sub), 2) == 0
    for i in range(keep_ref.shape[0]):
        mine, theirs = keep_ref[i], recv_ref[i]
        early = jnp.where(first, mine, theirs)
        late = jnp.where(first, theirs, mine)
        out_refs[i // 2][i % 2] = compose(late, early)


def group_kernel(n_sub, r0, r1, r2, r3, after_ref, total_map_ref, total_add_ref, ahead_ref, held):
    rank = my_rank(n_sub)
    chip = lax.rem(rank // 2, CHIPS)
    for slot, ref in enumerate((r0, r1, r2, r3)):
        held[chip ^ slot] = ref[...]
    for place in range(r0.shape[0]):
        one = held[0, place]
        two = compose(held[1, place], one)
        upper = compose(held[3, place], held[2, place])
        total = compose(upper, two)
        total_map_ref[place] = total[:, :D]
        total_add_ref[place] = total[:, D:]
        ahead_ref[place, 0] = one
        ahead_ref[place, 1] = two
        ahead_ref[place, 2] = compose(held[2, place], two)


def step_kernel(map_ref, add_ref, state_ref, out_ref):
    for place in range(map_ref.shape[0]):
        out_ref[place] = add_ref[place] + mm3(map_ref[place], state_ref[place])


def spread_kernel(n_sub, ahead_ref, state_ref, o0, o1, o2, o3, held):
    rank = my_rank(n_sub)
    chip = lax.rem(rank // 2, CHIPS)
    for place in range(state_ref.shape[0]):
        state = state_ref[place]
        held[0, place] = state
        for i in range(CHIPS - 1):
            held[i + 1, place] = (
                mm3(ahead_ref[place, i, :, :D], state) + ahead_ref[place, i, :, D:]
            )
    for slot, ref in enumerate((o0, o1, o2, o3)):
        ref[...] = held[chip ^ slot]


def readout_kernel(n_sub, lengths_ref, q_ref, k_ref, v_ref, decay_ref, rate_ref, *refs):
    n = len(PHASES)
    read_refs = refs[3 * n :]
    core = lax.rem(my_rank(n_sub), 2)
    seg_row, seg_col, before = token_masks(lengths_ref, n_sub)
    lower = (iota(0) >= iota(1)) & (seg_row == seg_col)
    reaches_row = (seg_row == before).astype(f32)
    reaches_col = (seg_col == before).astype(f32)
    for phase, slots in enumerate(PHASES):
        keys = key_heads(n_sub, slots)
        heads = value_heads(keys)
        sum_row, sum_col, rate_row, _ = gates(heads, decay_ref, rate_ref)
        for j in range(len(keys)):
            key = columns(k_ref, keys[j])
            key_t = key.T
            n_col, n_row = key_norms(key, key_t)
            query = columns(q_ref, keys[j])
            wide = query.astype(f32)
            q_col = lax.rsqrt(jnp.sum(wide * wide, axis=1, keepdims=True) + 1e-06)
            cross = mm(query, key_t) * n_row
            for part in range(2):
                i = 2 * j + part
                s_row, s_col = sum_row[i : i + 1, :], sum_col[:, i : i + 1]
                b_row = rate_row[i : i + 1, :]
                between = jnp.exp(jnp.minimum(s_col - s_row, 0.0))
                scores = jnp.where(lower, between * cross * q_col, 0.0)
                mixed = mm3(scores, refs[phase][i])
                from_row = jnp.exp(s_row) * reaches_row
                from_col = jnp.exp(s_col) * reaches_col
                fresh = mm2(mixed * b_row, columns(v_ref, heads[i]))
                through = wide * (from_col * q_col) - mm2(mixed * (b_row * from_row * n_row), key)
                read_refs[phase][i] = jnp.concatenate([through, fresh], axis=1)

    @pl.when(core == 1)
    def _():
        for phase in range(n):
            read_ref = read_refs[phase]
            half = read_ref.shape[0] // 2
            for i in range(2 * half):
                source = refs[n + phase] if i < half else refs[2 * n + phase]
                read = read_ref[i]
                both = mm3(read[:, :D], source[i % half])
                read_ref[i, :, :D] = both[:, :D]
                read_ref[i, :, D:] = both[:, D:] + read[:, D:]


def output_kernel(n_sub, gain_ref, *refs):
    read_refs, states, out_ref = refs[: len(PHASES)], refs[len(PHASES) : -1], refs[-1]
    gain = gain_ref[...]
    for phase, slots in enumerate(PHASES):
        heads = value_heads(key_heads(n_sub, slots))
        for i, h in enumerate(heads):
            side, place = divmod(i, 2 * len(slots))
            state = states[side * CHIPS + slots[place // 2]][place % 2]
            read = read_refs[phase][i]
            raw = mm3(read[:, :D], state) + read[:, D:]
            scale = lax.rsqrt(jnp.mean(raw * raw, axis=1, keepdims=True) + 1e-06)
            out_ref[:, pl.ds(pl.multiple_of(h * D, D), D)] = (raw * scale * gain).astype(bf16)


def call(kernel, outs, args, scratch=(), specs=None, flops=0, name=None, vmem=32):
    moved = sum(a.size * a.dtype.itemsize for a in args)
    moved += sum(math.prod(o.shape) * o.dtype.itemsize for o in jax.tree.leaves(outs))
    return pl.pallas_call(
        kernel,
        out_shape=outs,
        in_specs=[VMEM] * len(args) if specs is None else specs,
        out_specs=[VMEM] * len(outs) if isinstance(outs, tuple) else VMEM,
        scratch_shapes=list(scratch),
        compiler_params=pltpu.CompilerParams(vmem_limit_bytes=vmem * 2**20),
        cost_estimate=pl.CostEstimate(flops=flops, bytes_accessed=moved, transcendentals=0),
        name=name,
    )(*args)


def like(*shape):
    return jax.ShapeDtypeStruct(shape, f32)


def on_device(
    n_dev,
    n_sub,
    queries,
    key_vectors,
    values,
    log_decay,
    write_rate,
    passage_lengths,
    norm_gain,
):
    assert values.shape[0] == BLOCK
    tokens = n_dev * BLOCK
    longest = LONGEST.get(tokens, tokens)
    reach = min(-(-longest // (GROUP * BLOCK)), n_dev // GROUP)
    n = 2
    swap_pairs = [(i, i ^ 1) for i in range(n_dev)]
    next_pairs = [(i, i + GROUP) for i in range(n_dev - GROUP)]

    def chip_pairs(slot):
        return [(i, i ^ (2 * slot)) for i in range(n_dev)]

    def permute(x, pairs):
        return lax.ppermute(x, AXES, pairs)

    step = 2 * BLOCK**3
    inverses, recvs, extras, got = [], [], [], [None] * CHIPS
    inputs = (passage_lengths, key_vectors, values, log_decay, write_rate)
    after = []
    for phase, slots in enumerate(PHASES):
        count = 4 * len(slots)
        halves = pltpu.VMEM((count // 2, D, 2 * D), f32)
        scratch, specs = (), [SMEM] + [VMEM] * 4
        placed = inputs
        if phase == 0:
            placed = [pltpu.with_memory_space_constraint(x, pltpu.HBM) for x in inputs]
            specs = [HBM] * 5
            scratch = [pltpu.SMEM(passage_lengths.shape, jnp.int32)]
            scratch += [pltpu.VMEM(x.shape, x.dtype) for x in inputs[1:]]
            scratch += [pltpu.SemaphoreType.DMA((5,))]
        keep, send, inverse = call(
            functools.partial(maps_kernel, slots, n_sub),
            (halves, halves, pltpu.VMEM((count, BLOCK, BLOCK), f32)),
            (*placed, *after),
            scratch=scratch,
            specs=specs + [ANY] * len(after),
            flops=count * 44 * step,
            name="maps",
        )
        recv = permute(send, swap_pairs)
        inverses.append(inverse)
        recvs.append(recv)
        extras.append(permute(keep, swap_pairs))
        outs = call(
            functools.partial(chip_kernel, n_sub),
            (like(n, D, 2 * D),) * len(slots),
            (keep, recv),
            flops=count * 3 * step,
            name="chip",
        )
        after = [outs[0]]
        for slot, out in zip(slots, outs):
            got[slot] = permute(out, chip_pairs(slot)) if slot else out
    read = call(
        functools.partial(readout_kernel, n_sub),
        tuple(like(4 * len(slots), BLOCK, 2 * D) for slots in PHASES),
        (
            passage_lengths,
            queries,
            key_vectors,
            values,
            log_decay,
            write_rate,
            *inverses,
            *recvs,
            *extras,
        ),
        specs=[SMEM] + [VMEM] * (5 + 3 * len(PHASES)),
        flops=16 * 13 * step,
        name="readout",
    )
    total_map, total_add, ahead = call(
        functools.partial(group_kernel, n_sub),
        (like(n, D, D), like(n, D, D), like(n, 3, D, 2 * D)),
        (*got, read[0]),
        specs=[VMEM] * CHIPS + [ANY],
        scratch=(pltpu.VMEM((CHIPS, n, D, 2 * D), f32),),
        flops=n * 24 * step,
        name="group",
    )
    state = total_add
    for _ in range(reach - 1):
        state = permute(state, next_pairs)
        state = call(
            step_kernel,
            like(n, D, D),
            (total_map, total_add, state),
            flops=n * 3 * step,
            name="step",
        )
    state = permute(state, next_pairs)
    outs = call(
        functools.partial(spread_kernel, n_sub),
        (like(n, D, D),) * CHIPS,
        (ahead, state),
        scratch=(pltpu.VMEM((CHIPS, n, D, D), f32),),
        flops=n * 9 * step,
        name="spread",
    )
    own = [outs[0]] + [permute(outs[slot], chip_pairs(slot)) for slot in range(1, CHIPS)]
    other = [permute(x, swap_pairs) for x in own]
    return call(
        functools.partial(output_kernel, n_sub),
        jax.ShapeDtypeStruct((BLOCK, VALUE_HEADS * D), bf16),
        (norm_gain.reshape(1, D), *read, *own, *other),
        flops=16 * 3 * step,
        name="output",
    )


def solution(mesh):
    n_sub = mesh.shape["sub"]
    n_dev = mesh.shape["seq"] * n_sub
    tokens = P(AXES, None)
    heads = P(None, AXES)
    return jax.shard_map(
        functools.partial(on_device, n_dev, n_sub),
        mesh=mesh,
        in_specs=(tokens, tokens, tokens, heads, heads, P(), P()),
        out_specs=tokens,
        check_vma=False,
    )
```

```python
import functools
import math

import jax
import jax.numpy as jnp
from jax import lax
from jax.experimental import pallas as pl
from jax.experimental.pallas import tpu as pltpu
from jax.sharding import PartitionSpec as P

D = 128
VALUE_HEADS = 16
HK = 8
BLOCK = 128
AXES = ("seq", "sub")
CHIPS = 4
GROUP = 2 * CHIPS
LONGEST = {4096: 2048, 65536: 8192}

f32 = jnp.float32
bf16 = jnp.bfloat16
VMEM = pl.BlockSpec(memory_space=pltpu.VMEM)
ANY = pl.BlockSpec(memory_space=pl.ANY)
HBM = pl.BlockSpec(memory_space=pltpu.HBM)


def my_rank(n_sub):
    return lax.axis_index("seq") * n_sub + lax.axis_index("sub")


def mm(a, b):
    return lax.dot_general(a, b, (((1,), (0,)), ((), ())), preferred_element_type=f32)


def mm_nt(a, b, precision=None):
    return lax.dot_general(
        a, b, (((1,), (1,)), ((), ())), preferred_element_type=f32, precision=precision
    )


def split(x):
    high = x.astype(bf16)
    return high, (x - high.astype(f32)).astype(bf16)


def across(high, low):
    return jnp.concatenate([high, low], axis=1)


def square(high, low):
    wide = across(high, low)
    return jnp.concatenate([wide, wide], axis=0)


def left(x):
    return across(*split(x))


def right(x):
    return square(*split(x))


def fold(x):
    half = x.shape[1] // 2
    return x[:, :half] + x[:, half:]


def mm_tall(a, b):
    rows = a[0].shape[0]
    out = mm(jnp.concatenate(a, axis=0), across(*b))
    return out[:rows, :D] + (out[:rows, D:] + out[rows:, :D])


def mm_half(a, b):
    rows = a[0].shape[0]
    out = mm(jnp.concatenate(a, axis=0), b)
    return out[:rows] + out[rows:]


def mm3(a, b):
    return fold(mm(left(a), right(b)))


def mm2(a, b):
    return mm(left(a), twice(b))


def twice(x):
    return jnp.concatenate([x, x], axis=0)


def compose(later, early):
    both = mm3(later[:, :D], early)
    return jnp.concatenate([both[:, :D], both[:, D:] + later[:, D:]], axis=1)


def iota(axis):
    return lax.broadcasted_iota(jnp.int32, (BLOCK, BLOCK), axis)


def token_masks(lengths_ref, n_sub):
    first = my_rank(n_sub) * BLOCK
    row_at = first + lax.broadcasted_iota(jnp.int32, (1, BLOCK), 1)
    col_at = first + lax.broadcasted_iota(jnp.int32, (BLOCK, 1), 0)

    def one(i, carried):
        start, row, col, before = carried
        row = row + (row_at >= start).astype(jnp.int32)
        col = col + (col_at >= start).astype(jnp.int32)
        before = before + (first > start).astype(jnp.int32)
        return start + lengths_ref[i], row, col, before

    zero = jnp.int32(0)
    _, row, col, before = lax.fori_loop(
        0,
        lengths_ref.shape[0],
        one,
        (zero, jnp.zeros((1, BLOCK), jnp.int32), jnp.zeros((BLOCK, 1), jnp.int32), zero),
    )
    return row, col, before


def gates(heads, decay_ref, rate_ref):
    decay = jnp.concatenate([decay_ref[pl.ds(h, 1), :] for h in heads], axis=0)
    rate_row = jnp.concatenate([rate_ref[pl.ds(h, 1), :] for h in heads], axis=0)
    lower = (iota(0) >= iota(1)).astype(f32)
    eye = (iota(0) == iota(1)).astype(f32)
    highest = lax.Precision.HIGHEST
    sum_row = mm_nt(decay, lower, highest)
    sum_col = mm_nt(lower, decay, highest)
    rate_col = mm_nt(eye, rate_row, highest)
    return sum_row, sum_col, rate_row, rate_col


def columns(ref, at):
    return ref[:, pl.ds(pl.multiple_of(at * D, D), D)]


def key_heads(n_sub, side):
    rank = my_rank(n_sub)
    core, chip = lax.rem(rank, 2), lax.rem(rank // 2, CHIPS)
    return [CHIPS * (core ^ side) + (chip ^ slot) for slot in range(CHIPS)]


def value_heads(keys):
    return [2 * j + part for j in keys for part in range(2)]


def key_norms(key, key_t):
    wide = key.astype(f32)
    col = lax.rsqrt(jnp.sum(wide * wide, axis=1, keepdims=True) + 1e-06)
    wide_t = key_t.astype(f32)
    row = lax.rsqrt(jnp.sum(wide_t * wide_t, axis=0, keepdims=True) + 1e-06)
    return col, row


def odd_rows(x, size):
    return jnp.concatenate([x[i : i + size] for i in range(size, BLOCK, 2 * size)], axis=0)


def with_odd_rows(x, rows, size):
    pieces = []
    for i in range(0, BLOCK // 2, size):
        pieces += [x[2 * i : 2 * i + size], rows[i : i + size]]
    return jnp.concatenate(pieces, axis=0)


def invert(systems, apart):
    near = apart < 16
    eye = (apart == 0).astype(f32)
    solved = [eye - jnp.where(near, n, 0.0) for n in systems]
    parts = [split(n) for n in systems]
    near = near.astype(f32).astype(bf16)
    powers = [(high * near, low * near) for high, low in parts]
    powers = [split(fold(mm(across(*n), square(*n)))) for n in powers]
    for last in (False, False, True):
        if last:
            solved = [s + fold(mm(left(s), square(*n))) for s, n in zip(solved, powers)]
        else:
            both = [
                fold(mm(jnp.concatenate([across(*n), left(s)], axis=0), square(*n)))
                for n, s in zip(powers, solved)
            ]
            powers = [split(x[:BLOCK]) for x in both]
            solved = [s + x[BLOCK:] for s, x in zip(solved, both)]
    size = 16
    zero = jnp.zeros((BLOCK, BLOCK), bf16)
    while size < BLOCK:
        band = (apart >= size) & (apart < 2 * size)
        band = odd_rows(band.astype(f32), size).astype(bf16)
        pairs = [split(s) for s in solved]
        products = [
            split(mm_tall([odd_rows(p, size) * band for p in n], s))
            for n, s in zip(parts, pairs)
        ]
        fulls = [[with_odd_rows(zero, p, size) for p in u] for u in products]
        rows = [mm_tall([odd_rows(p, size) for p in s], u) for s, u in zip(pairs, fulls)]
        solved = [
            with_odd_rows(s, odd_rows(s, size) - r, size) for s, r in zip(solved, rows)
        ]
        size = 2 * size
    return solved


def first_maps_kernel(n_sub, *refs):
    sources, outs, (gain_ref, lengths_ref, sems) = refs[:6], refs[6:14], refs[14:]
    row_ref, col_ref = outs[6:]
    targets = (lengths_ref, *outs[2:6], gain_ref)
    copies = [
        pltpu.make_async_copy(a, b, sems.at[i]) for i, (a, b) in enumerate(zip(sources, targets))
    ]
    for copy in copies:
        copy.start()
    copies[0].wait()
    row, col, before = token_masks(lengths_ref, n_sub)
    row_ref[0:1] = row
    row_ref[1:2] = jnp.zeros_like(row) + before
    col_ref[...] = jnp.zeros((BLOCK, BLOCK), jnp.int32) + col
    for i in (1, 3, 4, 5):
        copies[i].wait()
    make_maps(1, n_sub, *outs[2:], *outs[:2], copies[2].wait)


def second_maps_kernel(n_sub, *refs):
    make_maps(0, n_sub, *refs, lambda: None)


def make_maps(
    side, n_sub, k_ref, v_ref, decay_ref, rate_ref, row_ref, col_ref, map_ref, inverse_ref, values_in
):
    keys = key_heads(n_sub, side)
    heads = value_heads(keys)
    seg_row, before = row_ref[0:1], row_ref[1:2]
    seg_col = col_ref[:, 0:1]
    sum_row, sum_col, rate_row, rate_col = gates(heads, decay_ref, rate_ref)
    apart = iota(0) ^ iota(1)
    strict = (iota(0) > iota(1)) & (seg_row == col_ref[...])
    eye = (apart == 0).astype(f32)
    reaches = (seg_row == before).astype(f32)
    last = seg_row[:, BLOCK - 1 :]
    ends_col = (seg_col == last).astype(f32)

    systems, details = [], []
    for j, key_head in enumerate(keys):
        key = columns(k_ref, key_head)
        key_t = key.T
        n_col, n_row = key_norms(key, key_t)
        gram = mm(key, key_t) * n_row
        for i in (2 * j, 2 * j + 1):
            s_row, s_col = sum_row[i : i + 1, :], sum_col[:, i : i + 1]
            b_row, b_col = rate_row[i : i + 1, :], rate_col[:, i : i + 1]
            between = jnp.exp(jnp.minimum(s_col - s_row, 0.0))
            systems.append(jnp.where(strict, between * gram * (b_col * n_col), 0.0))
            from_row = jnp.exp(s_row) * reaches
            end = jnp.exp(s_col[BLOCK - 1 :, :] - s_col) * ends_col * n_col
            details.append((key, key_t, n_row, b_row, from_row, end))
    solved = invert(systems, apart)
    values_in()
    for i, (key, key_t, n_row, b_row, from_row, end) in enumerate(details):
        inverse_ref[i] = solved[i]
        middle = solved[i] * end
        wy = mm_half(split(middle * (b_row * from_row * n_row)), key)
        fresh = mm_half(split(middle * b_row), columns(v_ref, heads[i]))
        high, low = split(across(wy, fresh))
        both = mm(across(key_t, key_t), jnp.concatenate([high, low], axis=0))
        map_ref[i, :, :D] = from_row[:, BLOCK - 1 :] * eye - both[:, :D]
        map_ref[i, :, D:] = both[:, D:]


def chip_kernel(n_sub, keep_ref, recv_ref, *out_refs):
    first = lax.rem(my_rank(n_sub), 2) == 0
    for i in range(keep_ref.shape[0]):
        mine, theirs = keep_ref[i], recv_ref[i]
        early = jnp.where(first, mine, theirs)
        late = jnp.where(first, theirs, mine)
        out_refs[i // 2][i % 2] = compose(late, early)


def group_kernel(n_sub, r0, r1, r2, r3, after_ref, add_ref, lower_ref, upper_ref, third_ref, held):
    chip = lax.rem(my_rank(n_sub) // 2, CHIPS)
    for slot, ref in enumerate((r0, r1, r2, r3)):
        held[chip ^ slot] = ref[...]
    for place in range(r0.shape[0]):
        one, third = held[0, place], held[2, place]
        two = compose(held[1, place], one)
        upper = compose(held[3, place], third)
        add_ref[place] = mm3(upper[:, :D], two[:, D:]) + upper[:, D:]
        lower_ref[place, 0] = one
        lower_ref[place, 1] = two
        upper_ref[place] = upper
        third_ref[place] = third


def ahead_kernel(lower_ref, upper_ref, third_ref, map_ref, ahead_ref):
    for place in range(upper_ref.shape[0]):
        two = lower_ref[place, 1]
        map_ref[place] = mm3(upper_ref[place, :, :D], two[:, :D])
        ahead_ref[place, 0] = lower_ref[place, 0]
        ahead_ref[place, 1] = two
        ahead_ref[place, 2] = compose(third_ref[place], two)


def step_kernel(map_ref, add_ref, state_ref, out_ref):
    for place in range(map_ref.shape[0]):
        out_ref[place] = add_ref[place] + mm3(map_ref[place], state_ref[place])


def spread_kernel(n_sub, ahead_ref, state_ref, o0, o1, o2, o3, held):
    rank = my_rank(n_sub)
    chip = lax.rem(rank // 2, CHIPS)
    for place in range(state_ref.shape[0]):
        state = state_ref[place]
        held[0, place] = state
        for i in range(CHIPS - 1):
            held[i + 1, place] = (
                mm3(ahead_ref[place, i, :, :D], state) + ahead_ref[place, i, :, D:]
            )
    for slot, ref in enumerate((o0, o1, o2, o3)):
        ref[...] = held[chip ^ slot]


def readout_kernel(n_sub, q_ref, k_ref, v_ref, decay_ref, rate_ref, row_ref, col_ref, *refs):
    inverse_refs, early_refs, read_refs = refs[:2], refs[2:4], refs[4:]
    core = lax.rem(my_rank(n_sub), 2)
    seg_row, before = row_ref[0:1], row_ref[1:2]
    lower = (iota(0) >= iota(1)) & (seg_row == col_ref[...])
    reaches_row = (seg_row == before).astype(f32)
    reaches_col = (col_ref[:, 0:1] == before[:, 0:1]).astype(f32)
    for side in range(2):
        keys = key_heads(n_sub, side)
        heads = value_heads(keys)
        sum_row, sum_col, rate_row, _ = gates(heads, decay_ref, rate_ref)
        for j, key_head in enumerate(keys):
            key = columns(k_ref, key_head)
            key_t = key.T
            n_col, n_row = key_norms(key, key_t)
            query = columns(q_ref, key_head)
            wide = query.astype(f32)
            q_col = lax.rsqrt(jnp.sum(wide * wide, axis=1, keepdims=True) + 1e-06)
            cross = mm(query, key_t) * n_row
            for i in (2 * j, 2 * j + 1):
                s_row, s_col = sum_row[i : i + 1, :], sum_col[:, i : i + 1]
                b_row = rate_row[i : i + 1, :]
                between = jnp.exp(jnp.minimum(s_col - s_row, 0.0))
                scores = jnp.where(lower, between * cross * q_col, 0.0)
                mixed = mm3(scores, inverse_refs[side][i])
                from_row = jnp.exp(s_row) * reaches_row
                from_col = jnp.exp(s_col) * reaches_col
                fresh = mm2(mixed * b_row, columns(v_ref, heads[i]))
                through = wide * (from_col * q_col) - mm2(mixed * (b_row * from_row * n_row), key)
                read_refs[side][i] = across(through, fresh)

    @pl.when(core == 1)
    def _():
        for early_ref, read_ref in zip(early_refs, read_refs):
            for i in range(VALUE_HEADS // 2):
                read = read_ref[i]
                both = mm3(read[:, :D], early_ref[i])
                read_ref[i, :, :D] = both[:, :D]
                read_ref[i, :, D:] = both[:, D:] + read[:, D:]


def normed(read, state, gain):
    raw = mm3(read[:, :D], state) + read[:, D:]
    scale = lax.rsqrt(jnp.mean(raw * raw, axis=1, keepdims=True) + 1e-06)
    return (raw * scale * gain).astype(bf16)


def early_output_kernel(gain_ref, *refs):
    read_refs, states, out_ref = refs[:2], refs[2:-1], refs[-1]
    for i in range(VALUE_HEADS - 2):
        side, at = divmod(i, VALUE_HEADS // 2)
        out_ref[i] = normed(read_refs[side][at], states[i // 2][at % 2], gain_ref[...])


def output_kernel(n_sub, gain_ref, read_ref, state_ref, early_ref, out_ref):
    heads = value_heads(key_heads(n_sub, 0)) + value_heads(key_heads(n_sub, 1))
    for i, h in enumerate(heads):
        if i < VALUE_HEADS - 2:
            out = early_ref[i]
        else:
            out = normed(read_ref[i - VALUE_HEADS // 2], state_ref[i % 2], gain_ref[...])
        out_ref[:, pl.ds(pl.multiple_of(h * D, D), D)] = out


def call(kernel, outs, args, scratch=(), specs=None, flops=0, name=None):
    moved = sum(a.size * a.dtype.itemsize for a in args)
    moved += sum(math.prod(o.shape) * o.dtype.itemsize for o in jax.tree.leaves(outs))
    return pl.pallas_call(
        kernel,
        out_shape=outs,
        in_specs=[VMEM] * len(args) if specs is None else specs,
        out_specs=[VMEM] * len(outs) if isinstance(outs, tuple) else VMEM,
        scratch_shapes=list(scratch),
        compiler_params=pltpu.CompilerParams(vmem_limit_bytes=32 * 2**20),
        cost_estimate=pl.CostEstimate(flops=flops, bytes_accessed=moved, transcendentals=0),
        name=name,
    )(*args)


def like(*shape):
    return jax.ShapeDtypeStruct(shape, f32)


def on_device(
    n_dev,
    n_sub,
    queries,
    key_vectors,
    values,
    log_decay,
    write_rate,
    passage_lengths,
    norm_gain,
):
    assert values.shape[0] == BLOCK
    tokens = n_dev * BLOCK
    longest = LONGEST.get(tokens, tokens)
    reach = min(-(-longest // (GROUP * BLOCK)), n_dev // GROUP)
    n = 2
    swap_pairs = [(i, i ^ 1) for i in range(n_dev)]
    next_pairs = [(i, i + GROUP) for i in range(n_dev - GROUP)]

    def chip_pairs(slot):
        return [(i, i ^ (2 * slot)) for i in range(n_dev)]

    def permute(x, pairs):
        return lax.ppermute(x, AXES, pairs)

    step = 2 * BLOCK**3
    half = VALUE_HEADS // 2
    made = (pltpu.VMEM((half, D, 2 * D), f32), pltpu.VMEM((half, BLOCK, BLOCK), f32))
    inputs = (
        passage_lengths,
        key_vectors,
        values,
        log_decay,
        write_rate,
        norm_gain.reshape(1, D),
    )
    send, send_inverse, *held, gain = call(
        functools.partial(first_maps_kernel, n_sub),
        (
            *made,
            *[pltpu.VMEM(x.shape, x.dtype) for x in inputs[1:5]],
            pltpu.VMEM((8, BLOCK), jnp.int32),
            pltpu.VMEM((BLOCK, BLOCK), jnp.int32),
            pltpu.VMEM((1, D), f32),
        ),
        [pltpu.with_memory_space_constraint(x, pltpu.HBM) for x in inputs],
        scratch=[
            pltpu.SMEM(passage_lengths.shape, jnp.int32),
            pltpu.SemaphoreType.DMA((6,)),
        ],
        specs=[HBM] * 6,
        flops=half * 44 * step,
        name="first_maps",
    )
    recv = permute(send, swap_pairs)
    keep, keep_inverse = call(
        functools.partial(second_maps_kernel, n_sub),
        made,
        held,
        flops=half * 44 * step,
        name="second_maps",
    )
    extra = permute(keep, swap_pairs)
    outs = call(
        functools.partial(chip_kernel, n_sub),
        (like(n, D, 2 * D),) * CHIPS,
        (keep, recv),
        flops=half * 6 * step,
        name="chip",
    )
    got = [outs[0]] + [permute(outs[slot], chip_pairs(slot)) for slot in range(1, CHIPS)]
    read = call(
        functools.partial(readout_kernel, n_sub),
        (like(half, BLOCK, 2 * D),) * 2,
        (queries, *held, keep_inverse, send_inverse, recv, extra),
        flops=16 * 13 * step,
        name="readout",
    )
    total_add, *held_maps = call(
        functools.partial(group_kernel, n_sub),
        (like(n, D, D), like(n, 2, D, 2 * D), like(n, D, 2 * D), like(n, D, 2 * D)),
        (*got, read[0]),
        specs=[VMEM] * CHIPS + [ANY],
        scratch=(pltpu.VMEM((CHIPS, n, D, 2 * D), f32),),
        flops=n * 15 * step,
        name="group",
    )
    total_map, ahead = call(
        ahead_kernel,
        (like(n, D, D), like(n, 3, D, 2 * D)),
        held_maps,
        flops=n * 9 * step,
        name="ahead",
    )
    state = total_add
    for _ in range(reach - 1):
        state = permute(state, next_pairs)
        state = call(
            step_kernel,
            like(n, D, D),
            (total_map, total_add, state),
            flops=n * 3 * step,
            name="step",
        )
    state = permute(state, next_pairs)
    outs = call(
        functools.partial(spread_kernel, n_sub),
        (like(n, D, D),) * CHIPS,
        (ahead, state),
        scratch=(pltpu.VMEM((CHIPS, n, D, D), f32),),
        flops=n * 9 * step,
        name="spread",
    )
    own = [outs[0]] + [permute(outs[slot], chip_pairs(slot)) for slot in range(1, CHIPS)]
    other = [permute(x, swap_pairs) for x in own]
    early = call(
        early_output_kernel,
        jax.ShapeDtypeStruct((VALUE_HEADS - 2, BLOCK, D), bf16),
        (gain, *read, *own, *other[:-1]),
        flops=14 * 3 * step,
        name="early_output",
    )
    return call(
        functools.partial(output_kernel, n_sub),
        jax.ShapeDtypeStruct((BLOCK, VALUE_HEADS * D), bf16),
        (gain, read[1], other[-1], early),
        flops=2 * 3 * step,
        name="output",
    )


def solution(mesh):
    n_sub = mesh.shape["sub"]
    n_dev = mesh.shape["seq"] * n_sub
    tokens = P(AXES, None)
    heads = P(None, AXES)
    return jax.shard_map(
        functools.partial(on_device, n_dev, n_sub),
        mesh=mesh,
        in_specs=(tokens, tokens, tokens, heads, heads, P(), P()),
        out_specs=tokens,
        check_vma=False,
    )
```

```python
import functools
import math

import jax
import jax.numpy as jnp
from jax import lax
from jax.experimental import pallas as pl
from jax.experimental.pallas import tpu as pltpu
from jax.sharding import PartitionSpec as P

D = 128
VALUE_HEADS = 16
HK = 8
BLOCK = 128
AXES = ("seq", "sub")
CHIPS = 4
GROUP = 2 * CHIPS
LONGEST = {4096: 2048, 65536: 8192}

f32 = jnp.float32
bf16 = jnp.bfloat16
VMEM = pl.BlockSpec(memory_space=pltpu.VMEM)
ANY = pl.BlockSpec(memory_space=pl.ANY)
HBM = pl.BlockSpec(memory_space=pltpu.HBM)


def my_rank(n_sub):
    return lax.axis_index("seq") * n_sub + lax.axis_index("sub")


def mm(a, b):
    return lax.dot_general(a, b, (((1,), (0,)), ((), ())), preferred_element_type=f32)


def mm_nt(a, b, precision=None):
    return lax.dot_general(
        a, b, (((1,), (1,)), ((), ())), preferred_element_type=f32, precision=precision
    )


def split(x):
    high = x.astype(bf16)
    return high, (x - high.astype(f32)).astype(bf16)


def across(high, low):
    return jnp.concatenate([high, low], axis=1)


def square(high, low):
    wide = across(high, low)
    return jnp.concatenate([wide, wide], axis=0)


def left(x):
    return across(*split(x))


def right(x):
    return square(*split(x))


def fold(x):
    half = x.shape[1] // 2
    return x[:, :half] + x[:, half:]


def mm_tall(a, b):
    rows = a[0].shape[0]
    out = mm(jnp.concatenate(a, axis=0), across(*b))
    return out[:rows, :D] + (out[:rows, D:] + out[rows:, :D])


def mm_long(a, b):
    return mm(
        jnp.concatenate([a[0], a[1], a[0]], axis=1), jnp.concatenate([b[0], b[0], b[1]], axis=0)
    )


def mm_half(a, b):
    rows = a[0].shape[0]
    out = mm(jnp.concatenate(a, axis=0), b)
    return out[:rows] + out[rows:]


def mm3(a, b):
    return fold(mm(left(a), right(b)))


def mm2(a, b):
    return mm(left(a), twice(b))


def twice(x):
    return jnp.concatenate([x, x], axis=0)


def compose(later, early):
    both = mm3(later[:, :D], early)
    return jnp.concatenate([both[:, :D], both[:, D:] + later[:, D:]], axis=1)


def iota(axis):
    return lax.broadcasted_iota(jnp.int32, (BLOCK, BLOCK), axis)


def token_masks(lengths_ref, n_sub):
    first = my_rank(n_sub) * BLOCK
    row_at = first + lax.broadcasted_iota(jnp.int32, (1, BLOCK), 1)
    col_at = first + lax.broadcasted_iota(jnp.int32, (BLOCK, 1), 0)

    def one(i, carried):
        start, row, col, before = carried
        row = row + (row_at >= start).astype(jnp.int32)
        col = col + (col_at >= start).astype(jnp.int32)
        before = before + (first > start).astype(jnp.int32)
        return start + lengths_ref[i], row, col, before

    zero = jnp.int32(0)
    _, row, col, before = lax.fori_loop(
        0,
        lengths_ref.shape[0],
        one,
        (zero, jnp.zeros((1, BLOCK), jnp.int32), jnp.zeros((BLOCK, 1), jnp.int32), zero),
    )
    return row, col, before


def gates(heads, decay_ref, rate_ref):
    decay = jnp.concatenate([decay_ref[pl.ds(h, 1), :] for h in heads], axis=0)
    rate_row = jnp.concatenate([rate_ref[pl.ds(h, 1), :] for h in heads], axis=0)
    lower = (iota(0) >= iota(1)).astype(f32)
    eye = (iota(0) == iota(1)).astype(f32)
    highest = lax.Precision.HIGHEST
    sum_row = mm_nt(decay, lower, highest)
    sum_col = mm_nt(lower, decay, highest)
    rate_col = mm_nt(eye, rate_row, highest)
    return sum_row, sum_col, rate_row, rate_col


def gates_of(side, *refs):
    at = slice(side * VALUE_HEADS // 2, (side + 1) * VALUE_HEADS // 2)
    sum_row, sum_col, rate_row, rate_col = refs
    return sum_row[at, :], sum_col[:, at], rate_row[at, :], rate_col[:, at]


def columns(ref, at):
    return ref[:, pl.ds(pl.multiple_of(at * D, D), D)]


def key_heads(n_sub, side):
    rank = my_rank(n_sub)
    core, chip = lax.rem(rank, 2), lax.rem(rank // 2, CHIPS)
    return [CHIPS * (core ^ side) + (chip ^ slot) for slot in range(CHIPS)]


def value_heads(keys):
    return [2 * j + part for j in keys for part in range(2)]


def key_norms(key, key_t):
    wide = key.astype(f32)
    col = lax.rsqrt(jnp.sum(wide * wide, axis=1, keepdims=True) + 1e-06)
    wide_t = key_t.astype(f32)
    row = lax.rsqrt(jnp.sum(wide_t * wide_t, axis=0, keepdims=True) + 1e-06)
    return col, row


def odd_rows(x, size):
    return jnp.concatenate([x[i : i + size] for i in range(size, BLOCK, 2 * size)], axis=0)


def with_odd_rows(x, rows, size):
    pieces = []
    for i in range(0, BLOCK // 2, size):
        pieces += [x[2 * i : 2 * i + size], rows[i : i + size]]
    return jnp.concatenate(pieces, axis=0)


def invert(systems, apart):
    near = apart < 16
    eye = (apart == 0).astype(f32)
    solved = [eye - jnp.where(near, n, 0.0) for n in systems]
    parts = [split(n) for n in systems]
    near = near.astype(f32).astype(bf16)
    powers = [(high * near, low * near) for high, low in parts]
    powers = [split(mm_long(n, n)) for n in powers]
    both = [fold(mm(jnp.concatenate([across(*n), left(s)], axis=0), square(*n))) for n, s in zip(powers, solved)]
    fourth = [odd_rows(x[:BLOCK], 8) for x in both]
    powers = [split(x[:BLOCK]) for x in both]
    solved = [s + x[BLOCK:] for s, x in zip(solved, both)]
    both = [
        fold(mm(jnp.concatenate([left(q), left(s)], axis=0), square(*n)))
        for q, n, s in zip(fourth, powers, solved)
    ]
    zero = jnp.zeros((BLOCK, BLOCK), f32)
    powers = [split(with_odd_rows(zero, x[: BLOCK // 2], 8)) for x in both]
    solved = [s + x[BLOCK // 2 :] for s, x in zip(solved, both)]
    rows = [odd_rows(s, 8) for s in solved]
    rows = [r + mm_long(split(r), n) for r, n in zip(rows, powers)]
    solved = [with_odd_rows(s, r, 8) for s, r in zip(solved, rows)]
    size = 16
    zero = jnp.zeros((BLOCK, BLOCK), bf16)
    while size < BLOCK:
        band = (apart >= size) & (apart < 2 * size)
        band = odd_rows(band.astype(f32), size).astype(bf16)
        pairs = [split(s) for s in solved]
        products = [
            split(mm_long([odd_rows(p, size) * band for p in n], s))
            for n, s in zip(parts, pairs)
        ]
        fulls = [[with_odd_rows(zero, p, size) for p in u] for u in products]
        rows = [mm_long([odd_rows(p, size) for p in s], u) for s, u in zip(pairs, fulls)]
        solved = [
            with_odd_rows(s, odd_rows(s, size) - r, size) for s, r in zip(solved, rows)
        ]
        size = 2 * size
    return solved


def first_maps_kernel(n_sub, *refs):
    sources, outs, refs = refs[:6], refs[6:16], refs[16:]
    gain_ref, lengths_ref, decay_ref, rate_ref, sems = refs
    row_ref, col_ref = outs[8:]
    targets = (lengths_ref, *outs[2:4], decay_ref, rate_ref, gain_ref)
    copies = [
        pltpu.make_async_copy(a, b, sems.at[i]) for i, (a, b) in enumerate(zip(sources, targets))
    ]
    for copy in copies:
        copy.start()
    copies[0].wait()
    row, col, before = token_masks(lengths_ref, n_sub)
    row_ref[0:1] = row
    row_ref[1:2] = jnp.zeros_like(row) + before
    col_ref[...] = jnp.zeros((BLOCK, BLOCK), jnp.int32) + col
    for i in (1, 3, 4, 5):
        copies[i].wait()
    heads = value_heads(key_heads(n_sub, 0)) + value_heads(key_heads(n_sub, 1))
    for ref, gate in zip(outs[4:8], gates(heads, decay_ref, rate_ref)):
        ref[...] = gate
    make_maps(1, n_sub, *outs[2:], *outs[:2], copies[2].wait)


def second_maps_kernel(n_sub, *refs):
    make_maps(0, n_sub, *refs, lambda: None)


def make_maps(
    side, n_sub, k_ref, v_ref, g0, g1, g2, g3, row_ref, col_ref, map_ref, inverse_ref, values_in
):
    keys = key_heads(n_sub, side)
    heads = value_heads(keys)
    seg_row, before = row_ref[0:1], row_ref[1:2]
    seg_col = col_ref[:, 0:1]
    sum_row, sum_col, rate_row, rate_col = gates_of(side, g0, g1, g2, g3)
    apart = iota(0) ^ iota(1)
    strict = (iota(0) > iota(1)) & (seg_row == col_ref[...])
    eye = (apart == 0).astype(f32)
    reaches = (seg_row == before).astype(f32)
    last = seg_row[:, BLOCK - 1 :]
    ends_col = (seg_col == last).astype(f32)

    systems, details = [], []
    for j, key_head in enumerate(keys):
        key = columns(k_ref, key_head)
        key_t = key.T
        n_col, n_row = key_norms(key, key_t)
        gram = mm(key, key_t) * n_row
        for i in (2 * j, 2 * j + 1):
            s_row, s_col = sum_row[i : i + 1, :], sum_col[:, i : i + 1]
            b_row, b_col = rate_row[i : i + 1, :], rate_col[:, i : i + 1]
            between = jnp.exp(jnp.minimum(s_col - s_row, 0.0))
            systems.append(jnp.where(strict, between * gram * (b_col * n_col), 0.0))
            from_row = jnp.exp(s_row) * reaches
            end = jnp.exp(s_col[BLOCK - 1 :, :] - s_col) * ends_col * n_col
            details.append((key, key_t, n_row, b_row, from_row, end))
    solved = invert(systems, apart)
    values_in()
    for i, (key, key_t, n_row, b_row, from_row, end) in enumerate(details):
        inverse_ref[i] = solved[i]
        through = fold(mm(key_t, across(*split(solved[i] * end))))
        mapped = mm_half(split(through * (b_row * from_row * n_row)), key)
        map_ref[i, :, :D] = from_row[:, BLOCK - 1 :] * eye - mapped
        map_ref[i, :, D:] = mm_half(split(through * b_row), columns(v_ref, heads[i]))


def chip_kernel(n_sub, keep_ref, recv_ref, *out_refs):
    first = lax.rem(my_rank(n_sub), 2) == 0
    for i in range(keep_ref.shape[0]):
        mine, theirs = keep_ref[i], recv_ref[i]
        early = jnp.where(first, mine, theirs)
        late = jnp.where(first, theirs, mine)
        out_refs[i // 2][i % 2] = compose(late, early)


def group_kernel(n_sub, r0, r1, r2, r3, after_ref, add_ref, lower_ref, upper_ref, third_ref, held):
    chip = lax.rem(my_rank(n_sub) // 2, CHIPS)
    for slot, ref in enumerate((r0, r1, r2, r3)):
        held[chip ^ slot] = ref[...]
    for place in range(r0.shape[0]):
        one, third = held[0, place], held[2, place]
        two = compose(held[1, place], one)
        upper = compose(held[3, place], third)
        add_ref[place] = mm3(upper[:, :D], two[:, D:]) + upper[:, D:]
        lower_ref[place, 0] = one
        lower_ref[place, 1] = two
        upper_ref[place] = upper
        third_ref[place] = third


def ahead_kernel(lower_ref, upper_ref, third_ref, map_ref, ahead_ref):
    for place in range(upper_ref.shape[0]):
        two = lower_ref[place, 1]
        map_ref[place] = mm3(upper_ref[place, :, :D], two[:, :D])
        ahead_ref[place, 0] = lower_ref[place, 0]
        ahead_ref[place, 1] = two
        ahead_ref[place, 2] = compose(third_ref[place], two)


def step_kernel(map_ref, add_ref, state_ref, out_ref):
    for place in range(map_ref.shape[0]):
        out_ref[place] = add_ref[place] + mm3(map_ref[place], state_ref[place])


def spread_kernel(n_sub, ahead_ref, state_ref, o0, o1, o2, o3, held):
    rank = my_rank(n_sub)
    chip = lax.rem(rank // 2, CHIPS)
    for place in range(state_ref.shape[0]):
        state = state_ref[place]
        held[0, place] = state
        for i in range(CHIPS - 1):
            held[i + 1, place] = (
                mm3(ahead_ref[place, i, :, :D], state) + ahead_ref[place, i, :, D:]
            )
    for slot, ref in enumerate((o0, o1, o2, o3)):
        ref[...] = held[chip ^ slot]


def readout_kernel(n_sub, q_ref, k_ref, v_ref, *refs):
    gate_refs, (row_ref, col_ref), refs = refs[:4], refs[4:6], refs[6:]
    inverse_refs, early_refs, read_refs = refs[:2], refs[2:4], refs[4:]
    core = lax.rem(my_rank(n_sub), 2)
    seg_row, before = row_ref[0:1], row_ref[1:2]
    lower = (iota(0) >= iota(1)) & (seg_row == col_ref[...])
    reaches_row = (seg_row == before).astype(f32)
    reaches_col = (col_ref[:, 0:1] == before[:, 0:1]).astype(f32)
    for side in range(2):
        keys = key_heads(n_sub, side)
        heads = value_heads(keys)
        sum_row, sum_col, rate_row, _ = gates_of(side, *gate_refs)
        for j, key_head in enumerate(keys):
            key = columns(k_ref, key_head)
            key_t = key.T
            n_col, n_row = key_norms(key, key_t)
            query = columns(q_ref, key_head)
            wide = query.astype(f32)
            q_col = lax.rsqrt(jnp.sum(wide * wide, axis=1, keepdims=True) + 1e-06)
            cross = mm(query, key_t) * n_row
            for i in (2 * j, 2 * j + 1):
                s_row, s_col = sum_row[i : i + 1, :], sum_col[:, i : i + 1]
                b_row = rate_row[i : i + 1, :]
                between = jnp.exp(jnp.minimum(s_col - s_row, 0.0))
                scores = jnp.where(lower, between * cross * q_col, 0.0)
                mixed = mm3(scores, inverse_refs[side][i])
                from_row = jnp.exp(s_row) * reaches_row
                from_col = jnp.exp(s_col) * reaches_col
                fresh = mm2(mixed * b_row, columns(v_ref, heads[i]))
                through = wide * (from_col * q_col) - mm2(mixed * (b_row * from_row * n_row), key)
                read_refs[side][i] = across(through, fresh)

    @pl.when(core == 1)
    def _():
        for early_ref, read_ref in zip(early_refs, read_refs):
            for i in range(VALUE_HEADS // 2):
                read = read_ref[i]
                both = mm3(read[:, :D], early_ref[i])
                read_ref[i, :, :D] = both[:, :D]
                read_ref[i, :, D:] = both[:, D:] + read[:, D:]


def normed(read, state, gain):
    raw = mm3(read[:, :D], state) + read[:, D:]
    scale = lax.rsqrt(jnp.mean(raw * raw, axis=1, keepdims=True) + 1e-06)
    return (raw * scale * gain).astype(bf16)


def early_output_kernel(gain_ref, *refs):
    read_refs, states, out_ref = refs[:2], refs[2:-1], refs[-1]
    for i in range(VALUE_HEADS - 2):
        side, at = divmod(i, VALUE_HEADS // 2)
        out_ref[i] = normed(read_refs[side][at], states[i // 2][at % 2], gain_ref[...])


def output_kernel(n_sub, gain_ref, read_ref, state_ref, early_ref, out_ref):
    heads = value_heads(key_heads(n_sub, 0)) + value_heads(key_heads(n_sub, 1))
    for i, h in enumerate(heads):
        if i < VALUE_HEADS - 2:
            out = early_ref[i]
        else:
            out = normed(read_ref[i - VALUE_HEADS // 2], state_ref[i % 2], gain_ref[...])
        out_ref[:, pl.ds(pl.multiple_of(h * D, D), D)] = out


def call(kernel, outs, args, scratch=(), specs=None, flops=0, name=None):
    moved = sum(a.size * a.dtype.itemsize for a in args)
    moved += sum(math.prod(o.shape) * o.dtype.itemsize for o in jax.tree.leaves(outs))
    return pl.pallas_call(
        kernel,
        out_shape=outs,
        in_specs=[VMEM] * len(args) if specs is None else specs,
        out_specs=[VMEM] * len(outs) if isinstance(outs, tuple) else VMEM,
        scratch_shapes=list(scratch),
        compiler_params=pltpu.CompilerParams(vmem_limit_bytes=32 * 2**20),
        cost_estimate=pl.CostEstimate(flops=flops, bytes_accessed=moved, transcendentals=0),
        name=name,
    )(*args)


def like(*shape):
    return jax.ShapeDtypeStruct(shape, f32)


def on_device(
    n_dev,
    n_sub,
    queries,
    key_vectors,
    values,
    log_decay,
    write_rate,
    passage_lengths,
    norm_gain,
):
    assert values.shape[0] == BLOCK
    tokens = n_dev * BLOCK
    longest = LONGEST.get(tokens, tokens)
    reach = min(-(-longest // (GROUP * BLOCK)), n_dev // GROUP)
    n = 2
    swap_pairs = [(i, i ^ 1) for i in range(n_dev)]
    next_pairs = [(i, i + GROUP) for i in range(n_dev - GROUP)]

    def chip_pairs(slot):
        return [(i, i ^ (2 * slot)) for i in range(n_dev)]

    def permute(x, pairs):
        return lax.ppermute(x, AXES, pairs)

    step = 2 * BLOCK**3
    half = VALUE_HEADS // 2
    made = (pltpu.VMEM((half, D, 2 * D), f32), pltpu.VMEM((half, BLOCK, BLOCK), f32))
    inputs = (
        passage_lengths,
        key_vectors,
        values,
        log_decay,
        write_rate,
        norm_gain.reshape(1, D),
    )
    send, send_inverse, *held, gain = call(
        functools.partial(first_maps_kernel, n_sub),
        (
            *made,
            *[pltpu.VMEM(x.shape, x.dtype) for x in inputs[1:3]],
            *[pltpu.VMEM(shape, f32) for shape in 2 * ((VALUE_HEADS, BLOCK), (BLOCK, VALUE_HEADS))],
            pltpu.VMEM((8, BLOCK), jnp.int32),
            pltpu.VMEM((BLOCK, BLOCK), jnp.int32),
            pltpu.VMEM((1, D), f32),
        ),
        [pltpu.with_memory_space_constraint(x, pltpu.HBM) for x in inputs],
        scratch=[
            pltpu.SMEM(passage_lengths.shape, jnp.int32),
            pltpu.VMEM(log_decay.shape, f32),
            pltpu.VMEM(write_rate.shape, f32),
            pltpu.SemaphoreType.DMA((6,)),
        ],
        specs=[HBM] * 6,
        flops=half * 44 * step,
        name="first_maps",
    )
    recv = permute(send, swap_pairs)
    keep, keep_inverse = call(
        functools.partial(second_maps_kernel, n_sub),
        made,
        held,
        flops=half * 44 * step,
        name="second_maps",
    )
    extra = permute(keep, swap_pairs)
    outs = call(
        functools.partial(chip_kernel, n_sub),
        (like(n, D, 2 * D),) * CHIPS,
        (keep, recv),
        flops=half * 6 * step,
        name="chip",
    )
    got = [outs[0]] + [permute(outs[slot], chip_pairs(slot)) for slot in range(1, CHIPS)]
    read = call(
        functools.partial(readout_kernel, n_sub),
        (like(half, BLOCK, 2 * D),) * 2,
        (queries, *held, keep_inverse, send_inverse, recv, extra),
        flops=16 * 13 * step,
        name="readout",
    )
    total_add, *held_maps = call(
        functools.partial(group_kernel, n_sub),
        (like(n, D, D), like(n, 2, D, 2 * D), like(n, D, 2 * D), like(n, D, 2 * D)),
        (*got, read[0]),
        specs=[VMEM] * CHIPS + [ANY],
        scratch=(pltpu.VMEM((CHIPS, n, D, 2 * D), f32),),
        flops=n * 15 * step,
        name="group",
    )
    total_map, ahead = call(
        ahead_kernel,
        (like(n, D, D), like(n, 3, D, 2 * D)),
        held_maps,
        flops=n * 9 * step,
        name="ahead",
    )
    state = total_add
    for _ in range(reach - 1):
        state = permute(state, next_pairs)
        state = call(
            step_kernel,
            like(n, D, D),
            (total_map, total_add, state),
            flops=n * 3 * step,
            name="step",
        )
    state = permute(state, next_pairs)
    outs = call(
        functools.partial(spread_kernel, n_sub),
        (like(n, D, D),) * CHIPS,
        (ahead, state),
        scratch=(pltpu.VMEM((CHIPS, n, D, D), f32),),
        flops=n * 9 * step,
        name="spread",
    )
    own = [outs[0]] + [permute(outs[slot], chip_pairs(slot)) for slot in range(1, CHIPS)]
    other = [permute(x, swap_pairs) for x in own]
    early = call(
        early_output_kernel,
        jax.ShapeDtypeStruct((VALUE_HEADS - 2, BLOCK, D), bf16),
        (gain, *read, *own, *other[:-1]),
        flops=14 * 3 * step,
        name="early_output",
    )
    return call(
        functools.partial(output_kernel, n_sub),
        jax.ShapeDtypeStruct((BLOCK, VALUE_HEADS * D), bf16),
        (gain, read[1], other[-1], early),
        flops=2 * 3 * step,
        name="output",
    )


def solution(mesh):
    n_sub = mesh.shape["sub"]
    n_dev = mesh.shape["seq"] * n_sub
    tokens = P(AXES, None)
    heads = P(None, AXES)
    return jax.shard_map(
        functools.partial(on_device, n_dev, n_sub),
        mesh=mesh,
        in_specs=(tokens, tokens, tokens, heads, heads, P(), P()),
        out_specs=tokens,
        check_vma=False,
    )
```

```python
import functools
import math

import jax
import jax.numpy as jnp
from jax import lax
from jax.experimental import pallas as pl
from jax.experimental.pallas import tpu as pltpu
from jax.sharding import PartitionSpec as P

D = 128
VALUE_HEADS = 16
HK = 8
BLOCK = 128
AXES = ("seq", "sub")
CHIPS = 4
GROUP = 2 * CHIPS
LONGEST = {4096: 2048, 65536: 8192}

f32 = jnp.float32
bf16 = jnp.bfloat16
VMEM = pl.BlockSpec(memory_space=pltpu.VMEM)
ANY = pl.BlockSpec(memory_space=pl.ANY)
HBM = pl.BlockSpec(memory_space=pltpu.HBM)


def my_rank(n_sub):
    return lax.axis_index("seq") * n_sub + lax.axis_index("sub")


def mm(a, b):
    return lax.dot_general(a, b, (((1,), (0,)), ((), ())), preferred_element_type=f32)


def mm_nt(a, b, precision=None):
    return lax.dot_general(
        a, b, (((1,), (1,)), ((), ())), preferred_element_type=f32, precision=precision
    )


def split(x):
    high = x.astype(bf16)
    return high, (x - high.astype(f32)).astype(bf16)


def across(high, low):
    return jnp.concatenate([high, low], axis=1)


def square(high, low):
    wide = across(high, low)
    return jnp.concatenate([wide, wide], axis=0)


def left(x):
    return across(*split(x))


def right(x):
    return square(*split(x))


def fold(x):
    half = x.shape[1] // 2
    return x[:, :half] + x[:, half:]


def mm_tall(a, b):
    rows = a[0].shape[0]
    out = mm(jnp.concatenate(a, axis=0), across(*b))
    return out[:rows, :D] + (out[:rows, D:] + out[rows:, :D])


def mm_long(a, b):
    return mm(
        jnp.concatenate([a[0], a[1], a[0]], axis=1), jnp.concatenate([b[0], b[0], b[1]], axis=0)
    )


def mm3(a, b):
    return fold(mm(left(a), right(b)))


def mm2(a, b):
    return mm(left(a), twice(b))


def twice(x):
    return jnp.concatenate([x, x], axis=0)


def compose(later, early):
    both = mm3(later[:, :D], early)
    return jnp.concatenate([both[:, :D], both[:, D:] + later[:, D:]], axis=1)


def iota(axis):
    return lax.broadcasted_iota(jnp.int32, (BLOCK, BLOCK), axis)


def token_masks(lengths_ref, n_sub):
    first = my_rank(n_sub) * BLOCK
    row_at = first + lax.broadcasted_iota(jnp.int32, (1, BLOCK), 1)
    col_at = first + lax.broadcasted_iota(jnp.int32, (BLOCK, 1), 0)

    def one(i, carried):
        start, row, col, before = carried
        row = row + (row_at >= start).astype(jnp.int32)
        col = col + (col_at >= start).astype(jnp.int32)
        before = before + (first > start).astype(jnp.int32)
        return start + lengths_ref[i], row, col, before

    zero = jnp.int32(0)
    _, row, col, before = lax.fori_loop(
        0,
        lengths_ref.shape[0],
        one,
        (zero, jnp.zeros((1, BLOCK), jnp.int32), jnp.zeros((BLOCK, 1), jnp.int32), zero),
    )
    return row, col, before


def gates(heads, decay_ref, rate_ref):
    decay = jnp.concatenate([decay_ref[pl.ds(h, 1), :] for h in heads], axis=0)
    rate_row = jnp.concatenate([rate_ref[pl.ds(h, 1), :] for h in heads], axis=0)
    lower = (iota(0) >= iota(1)).astype(f32)
    eye = (iota(0) == iota(1)).astype(f32)
    highest = lax.Precision.HIGHEST
    sum_row = mm_nt(decay, lower, highest)
    sum_col = mm_nt(lower, decay, highest)
    rate_col = mm_nt(eye, rate_row, highest)
    return sum_row, sum_col, rate_row, rate_col


def gates_of(side, *refs):
    at = slice(side * VALUE_HEADS // 2, (side + 1) * VALUE_HEADS // 2)
    sum_row, sum_col, rate_row, rate_col = refs
    return sum_row[at, :], sum_col[:, at], rate_row[at, :], rate_col[:, at]


def columns(ref, at):
    return ref[:, pl.ds(pl.multiple_of(at * D, D), D)]


def key_heads(n_sub, side):
    rank = my_rank(n_sub)
    core, chip = lax.rem(rank, 2), lax.rem(rank // 2, CHIPS)
    return [CHIPS * (core ^ side) + (chip ^ slot) for slot in range(CHIPS)]


def value_heads(keys):
    return [2 * j + part for j in keys for part in range(2)]


def key_norms(key, key_t):
    wide = key.astype(f32)
    col = lax.rsqrt(jnp.sum(wide * wide, axis=1, keepdims=True) + 1e-06)
    wide_t = key_t.astype(f32)
    row = lax.rsqrt(jnp.sum(wide_t * wide_t, axis=0, keepdims=True) + 1e-06)
    return col, row


def odd_rows(x, size):
    return jnp.concatenate([x[i : i + size] for i in range(size, BLOCK, 2 * size)], axis=0)


def with_odd_rows(x, rows, size):
    pieces = []
    for i in range(0, BLOCK // 2, size):
        pieces += [x[2 * i : 2 * i + size], rows[i : i + size]]
    return jnp.concatenate(pieces, axis=0)


def invert(systems, apart):
    near = apart < 16
    eye = (apart == 0).astype(f32)
    solved = [eye - jnp.where(near, n, 0.0) for n in systems]
    parts = [split(n) for n in systems]
    near = near.astype(f32).astype(bf16)
    powers = [(high * near, low * near) for high, low in parts]
    powers = [split(mm_long(n, n)) for n in powers]
    both = [fold(mm(jnp.concatenate([across(*n), left(s)], axis=0), square(*n))) for n, s in zip(powers, solved)]
    fourth = [odd_rows(x[:BLOCK], 8) for x in both]
    powers = [split(x[:BLOCK]) for x in both]
    solved = [s + x[BLOCK:] for s, x in zip(solved, both)]
    both = [
        fold(mm(jnp.concatenate([left(q), left(s)], axis=0), square(*n)))
        for q, n, s in zip(fourth, powers, solved)
    ]
    zero = jnp.zeros((BLOCK, BLOCK), f32)
    powers = [split(with_odd_rows(zero, x[: BLOCK // 2], 8)) for x in both]
    solved = [s + x[BLOCK // 2 :] for s, x in zip(solved, both)]
    rows = [odd_rows(s, 8) for s in solved]
    rows = [r + mm_long(split(r), n) for r, n in zip(rows, powers)]
    solved = [with_odd_rows(s, r, 8) for s, r in zip(solved, rows)]
    size = 16
    zero = jnp.zeros((BLOCK, BLOCK), bf16)
    while size < BLOCK:
        band = (apart >= size) & (apart < 2 * size)
        band = odd_rows(band.astype(f32), size).astype(bf16)
        pairs = [split(s) for s in solved]
        products = [
            split(mm_long([odd_rows(p, size) * band for p in n], s))
            for n, s in zip(parts, pairs)
        ]
        fulls = [[with_odd_rows(zero, p, size) for p in u] for u in products]
        rows = [mm_long([odd_rows(p, size) for p in s], u) for s, u in zip(pairs, fulls)]
        solved = [
            with_odd_rows(s, odd_rows(s, size) - r, size) for s, r in zip(solved, rows)
        ]
        size = 2 * size
    return solved


def first_maps_kernel(n_sub, *refs):
    sources, outs, refs = refs[:6], refs[6:16], refs[16:]
    gain_ref, lengths_ref, decay_ref, rate_ref, sems = refs
    row_ref, col_ref = outs[8:]
    targets = (lengths_ref, *outs[2:4], decay_ref, rate_ref, gain_ref)
    copies = [
        pltpu.make_async_copy(a, b, sems.at[i]) for i, (a, b) in enumerate(zip(sources, targets))
    ]
    for copy in copies:
        copy.start()
    copies[0].wait()
    row, col, before = token_masks(lengths_ref, n_sub)
    row_ref[0:1] = row
    row_ref[1:2] = jnp.zeros_like(row) + before
    col_ref[...] = jnp.zeros((BLOCK, BLOCK), jnp.int32) + col
    for i in (1, 3, 4, 5):
        copies[i].wait()
    heads = value_heads(key_heads(n_sub, 0)) + value_heads(key_heads(n_sub, 1))
    for ref, gate in zip(outs[4:8], gates(heads, decay_ref, rate_ref)):
        ref[...] = gate
    make_maps(1, n_sub, *outs[2:], *outs[:2], copies[2].wait)


def second_maps_kernel(n_sub, *refs):
    make_maps(0, n_sub, *refs, lambda: None)


def make_maps(
    side, n_sub, k_ref, v_ref, g0, g1, g2, g3, row_ref, col_ref, map_ref, inverse_ref, values_in
):
    keys = key_heads(n_sub, side)
    heads = value_heads(keys)
    seg_row, before = row_ref[0:1], row_ref[1:2]
    seg_col = col_ref[:, 0:1]
    sum_row, sum_col, rate_row, rate_col = gates_of(side, g0, g1, g2, g3)
    apart = iota(0) ^ iota(1)
    strict = (iota(0) > iota(1)) & (seg_row == col_ref[...])
    eye = (apart == 0).astype(f32)
    reaches = (seg_row == before).astype(f32)
    last = seg_row[:, BLOCK - 1 :]
    ends_col = (seg_col == last).astype(f32)

    systems, details = [], []
    for j, key_head in enumerate(keys):
        key = columns(k_ref, key_head)
        key_t = key.T
        n_col, n_row = key_norms(key, key_t)
        gram = mm(key, key_t) * n_row
        for i in (2 * j, 2 * j + 1):
            s_row, s_col = sum_row[i : i + 1, :], sum_col[:, i : i + 1]
            b_row, b_col = rate_row[i : i + 1, :], rate_col[:, i : i + 1]
            between = jnp.exp(jnp.minimum(s_col - s_row, 0.0))
            systems.append(jnp.where(strict, between * gram * (b_col * n_col), 0.0))
            from_row = jnp.exp(s_row) * reaches
            end = jnp.exp(s_col[BLOCK - 1 :, :] - s_col) * ends_col * n_col
            details.append((key, key_t, n_row, b_row, from_row, end))
    solved = invert(systems, apart)
    values_in()
    for i, (key, key_t, n_row, b_row, from_row, end) in enumerate(details):
        inverse_ref[i] = solved[i]
        through = fold(mm(key_t, across(*split(solved[i] * end))))
        mapped = mm2(through * (b_row * from_row * n_row), key)
        map_ref[i, :, :D] = from_row[:, BLOCK - 1 :] * eye - mapped
        map_ref[i, :, D:] = mm2(through * b_row, columns(v_ref, heads[i]))


def chip_kernel(n_sub, keep_ref, recv_ref, *out_refs):
    first = lax.rem(my_rank(n_sub), 2) == 0
    for i in range(keep_ref.shape[0]):
        mine, theirs = keep_ref[i], recv_ref[i]
        early = jnp.where(first, mine, theirs)
        late = jnp.where(first, theirs, mine)
        out_refs[i // 2][i % 2] = compose(late, early)


def group_kernel(n_sub, r0, r1, r2, r3, after_ref, add_ref, lower_ref, upper_ref, third_ref, held):
    chip = lax.rem(my_rank(n_sub) // 2, CHIPS)
    for slot, ref in enumerate((r0, r1, r2, r3)):
        held[chip ^ slot] = ref[...]
    for place in range(r0.shape[0]):
        one, third = held[0, place], held[2, place]
        two = compose(held[1, place], one)
        upper = compose(held[3, place], third)
        add_ref[place] = mm3(upper[:, :D], two[:, D:]) + upper[:, D:]
        lower_ref[place, 0] = one
        lower_ref[place, 1] = two
        upper_ref[place] = upper
        third_ref[place] = third


def ahead_kernel(lower_ref, upper_ref, third_ref, map_ref, ahead_ref):
    for place in range(upper_ref.shape[0]):
        two = lower_ref[place, 1]
        map_ref[place] = mm3(upper_ref[place, :, :D], two[:, :D])
        ahead_ref[place, 0] = lower_ref[place, 0]
        ahead_ref[place, 1] = two
        ahead_ref[place, 2] = compose(third_ref[place], two)


def step_kernel(map_ref, add_ref, state_ref, out_ref):
    for place in range(map_ref.shape[0]):
        out_ref[place] = add_ref[place] + mm3(map_ref[place], state_ref[place])


def spread_kernel(n_sub, ahead_ref, state_ref, o0, o1, o2, o3, held):
    rank = my_rank(n_sub)
    chip = lax.rem(rank // 2, CHIPS)
    for place in range(state_ref.shape[0]):
        state = state_ref[place]
        held[0, place] = state
        for i in range(CHIPS - 1):
            held[i + 1, place] = (
                mm3(ahead_ref[place, i, :, :D], state) + ahead_ref[place, i, :, D:]
            )
    for slot, ref in enumerate((o0, o1, o2, o3)):
        ref[...] = held[chip ^ slot]


def readout_kernel(n_sub, q_ref, k_ref, v_ref, *refs):
    gate_refs, (row_ref, col_ref), refs = refs[:4], refs[4:6], refs[6:]
    inverse_refs, early_refs, read_refs = refs[:2], refs[2:4], refs[4:]
    core = lax.rem(my_rank(n_sub), 2)
    seg_row, before = row_ref[0:1], row_ref[1:2]
    lower = (iota(0) >= iota(1)) & (seg_row == col_ref[...])
    reaches_row = (seg_row == before).astype(f32)
    reaches_col = (col_ref[:, 0:1] == before[:, 0:1]).astype(f32)
    for side in range(2):
        keys = key_heads(n_sub, side)
        heads = value_heads(keys)
        sum_row, sum_col, rate_row, _ = gates_of(side, *gate_refs)
        for j, key_head in enumerate(keys):
            key = columns(k_ref, key_head)
            key_t = key.T
            n_col, n_row = key_norms(key, key_t)
            query = columns(q_ref, key_head)
            wide = query.astype(f32)
            q_col = lax.rsqrt(jnp.sum(wide * wide, axis=1, keepdims=True) + 1e-06)
            cross = mm(query, key_t) * n_row
            for i in (2 * j, 2 * j + 1):
                s_row, s_col = sum_row[i : i + 1, :], sum_col[:, i : i + 1]
                b_row = rate_row[i : i + 1, :]
                between = jnp.exp(jnp.minimum(s_col - s_row, 0.0))
                scores = jnp.where(lower, between * cross * q_col, 0.0)
                mixed = mm3(scores, inverse_refs[side][i])
                from_row = jnp.exp(s_row) * reaches_row
                from_col = jnp.exp(s_col) * reaches_col
                fresh = mm2(mixed * b_row, columns(v_ref, heads[i]))
                through = wide * (from_col * q_col) - mm2(mixed * (b_row * from_row * n_row), key)
                read_refs[side][i] = across(through, fresh)

    @pl.when(core == 1)
    def _():
        for early_ref, read_ref in zip(early_refs, read_refs):
            for i in range(VALUE_HEADS // 2):
                read = read_ref[i]
                both = mm3(read[:, :D], early_ref[i])
                read_ref[i, :, :D] = both[:, :D]
                read_ref[i, :, D:] = both[:, D:] + read[:, D:]


def normed(read, state, gain):
    raw = mm3(read[:, :D], state) + read[:, D:]
    scale = lax.rsqrt(jnp.mean(raw * raw, axis=1, keepdims=True) + 1e-06)
    return (raw * scale * gain).astype(bf16)


def early_output_kernel(gain_ref, *refs):
    read_refs, states, out_ref = refs[:2], refs[2:-1], refs[-1]
    for i in range(VALUE_HEADS - 2):
        side, at = divmod(i, VALUE_HEADS // 2)
        out_ref[i] = normed(read_refs[side][at], states[i // 2][at % 2], gain_ref[...])


def output_kernel(n_sub, gain_ref, read_ref, state_ref, early_ref, out_ref):
    heads = value_heads(key_heads(n_sub, 0)) + value_heads(key_heads(n_sub, 1))
    for i, h in enumerate(heads):
        if i < VALUE_HEADS - 2:
            out = early_ref[i]
        else:
            out = normed(read_ref[i - VALUE_HEADS // 2], state_ref[i % 2], gain_ref[...])
        out_ref[:, pl.ds(pl.multiple_of(h * D, D), D)] = out


def call(kernel, outs, args, scratch=(), specs=None, flops=0, name=None):
    moved = sum(a.size * a.dtype.itemsize for a in args)
    moved += sum(math.prod(o.shape) * o.dtype.itemsize for o in jax.tree.leaves(outs))
    return pl.pallas_call(
        kernel,
        out_shape=outs,
        in_specs=[VMEM] * len(args) if specs is None else specs,
        out_specs=[VMEM] * len(outs) if isinstance(outs, tuple) else VMEM,
        scratch_shapes=list(scratch),
        compiler_params=pltpu.CompilerParams(vmem_limit_bytes=32 * 2**20),
        cost_estimate=pl.CostEstimate(flops=flops, bytes_accessed=moved, transcendentals=0),
        name=name,
    )(*args)


def like(*shape):
    return jax.ShapeDtypeStruct(shape, f32)


def on_device(
    n_dev,
    n_sub,
    queries,
    key_vectors,
    values,
    log_decay,
    write_rate,
    passage_lengths,
    norm_gain,
):
    assert values.shape[0] == BLOCK
    tokens = n_dev * BLOCK
    longest = LONGEST.get(tokens, tokens)
    reach = min(-(-longest // (GROUP * BLOCK)), n_dev // GROUP)
    n = 2
    swap_pairs = [(i, i ^ 1) for i in range(n_dev)]
    next_pairs = [(i, i + GROUP) for i in range(n_dev - GROUP)]

    def chip_pairs(slot):
        return [(i, i ^ (2 * slot)) for i in range(n_dev)]

    def permute(x, pairs):
        return lax.ppermute(x, AXES, pairs)

    step = 2 * BLOCK**3
    half = VALUE_HEADS // 2
    made = (pltpu.VMEM((half, D, 2 * D), f32), pltpu.VMEM((half, BLOCK, BLOCK), f32))
    inputs = (
        passage_lengths,
        key_vectors,
        values,
        log_decay,
        write_rate,
        norm_gain.reshape(1, D),
    )
    send, send_inverse, *held, gain = call(
        functools.partial(first_maps_kernel, n_sub),
        (
            *made,
            *[pltpu.VMEM(x.shape, x.dtype) for x in inputs[1:3]],
            *[pltpu.VMEM(shape, f32) for shape in 2 * ((VALUE_HEADS, BLOCK), (BLOCK, VALUE_HEADS))],
            pltpu.VMEM((8, BLOCK), jnp.int32),
            pltpu.VMEM((BLOCK, BLOCK), jnp.int32),
            pltpu.VMEM((1, D), f32),
        ),
        [pltpu.with_memory_space_constraint(x, pltpu.HBM) for x in inputs],
        scratch=[
            pltpu.SMEM(passage_lengths.shape, jnp.int32),
            pltpu.VMEM(log_decay.shape, f32),
            pltpu.VMEM(write_rate.shape, f32),
            pltpu.SemaphoreType.DMA((6,)),
        ],
        specs=[HBM] * 6,
        flops=half * 44 * step,
        name="first_maps",
    )
    recv = permute(send, swap_pairs)
    keep, keep_inverse = call(
        functools.partial(second_maps_kernel, n_sub),
        made,
        held,
        flops=half * 44 * step,
        name="second_maps",
    )
    extra = permute(keep, swap_pairs)
    outs = call(
        functools.partial(chip_kernel, n_sub),
        (like(n, D, 2 * D),) * CHIPS,
        (keep, recv),
        flops=half * 6 * step,
        name="chip",
    )
    got = [outs[0]] + [permute(outs[slot], chip_pairs(slot)) for slot in range(1, CHIPS)]
    read = call(
        functools.partial(readout_kernel, n_sub),
        (like(half, BLOCK, 2 * D),) * 2,
        (queries, *held, keep_inverse, send_inverse, recv, extra),
        flops=16 * 13 * step,
        name="readout",
    )
    total_add, *held_maps = call(
        functools.partial(group_kernel, n_sub),
        (like(n, D, D), like(n, 2, D, 2 * D), like(n, D, 2 * D), like(n, D, 2 * D)),
        (*got, read[0]),
        specs=[VMEM] * CHIPS + [ANY],
        scratch=(pltpu.VMEM((CHIPS, n, D, 2 * D), f32),),
        flops=n * 15 * step,
        name="group",
    )
    total_map, ahead = call(
        ahead_kernel,
        (like(n, D, D), like(n, 3, D, 2 * D)),
        held_maps,
        flops=n * 9 * step,
        name="ahead",
    )
    state = total_add
    for _ in range(reach - 1):
        state = permute(state, next_pairs)
        state = call(
            step_kernel,
            like(n, D, D),
            (total_map, total_add, state),
            flops=n * 3 * step,
            name="step",
        )
    state = permute(state, next_pairs)
    outs = call(
        functools.partial(spread_kernel, n_sub),
        (like(n, D, D),) * CHIPS,
        (ahead, state),
        scratch=(pltpu.VMEM((CHIPS, n, D, D), f32),),
        flops=n * 9 * step,
        name="spread",
    )
    own = [outs[0]] + [permute(outs[slot], chip_pairs(slot)) for slot in range(1, CHIPS)]
    other = [permute(x, swap_pairs) for x in own]
    early = call(
        early_output_kernel,
        jax.ShapeDtypeStruct((VALUE_HEADS - 2, BLOCK, D), bf16),
        (gain, *read, *own, *other[:-1]),
        flops=14 * 3 * step,
        name="early_output",
    )
    return call(
        functools.partial(output_kernel, n_sub),
        jax.ShapeDtypeStruct((BLOCK, VALUE_HEADS * D), bf16),
        (gain, read[1], other[-1], early),
        flops=2 * 3 * step,
        name="output",
    )


def solution(mesh):
    n_sub = mesh.shape["sub"]
    n_dev = mesh.shape["seq"] * n_sub
    tokens = P(AXES, None)
    heads = P(None, AXES)
    return jax.shard_map(
        functools.partial(on_device, n_dev, n_sub),
        mesh=mesh,
        in_specs=(tokens, tokens, tokens, heads, heads, P(), P()),
        out_specs=tokens,
        check_vma=False,
    )
```
